32 devices in a mesh: leaf: 4 (over y, core), front: 8 (over z, x).
Axes of the slice: x: 2, y: 2, z: 4, core: 2. Of those that a mesh axis runs over, the one named last changes fastest.
Arguments:
- leaf_inverse: bfloat16 [1024, 128, 128], P(('leaf', 'front')), may hold values from -0.5 to 0.5
- leaf_rhs: bfloat16 [1024, 128, 256], P(('leaf', 'front')), may hold values from -6 to 6
- off_blocks: bfloat16 [1024, 5, 128, 128], P(('leaf', 'front')), may hold values from -0.0546875 to 0.0546875
- block_rows: int32 [1024, 5], P(('leaf', 'front')), may hold values from 0 to 15
- fill_count: int32 [1024], P(('leaf', 'front')), may hold values from 1 to 5
- sep_rhs: bfloat16 [32, 128, 256], P(('leaf', 'front')), may hold values from -6 to 6
- panel_order: int32 [4, 8], P('leaf'), may hold values from 0 to 7, each once within a row
- sep_inverse: bfloat16 [32, 128, 1024], P(('leaf', 'front')), may hold values from -0.1875 to 0.1875
Outputs:
- leaf_solution: bfloat16 [1024, 128, 256], P(('leaf', 'front'))
- sep_forward: bfloat16 [32, 128, 256], P(('leaf', 'front'))
- sep_solution: float32 [32, 128, 256], P(('leaf', 'front'))
The draws below stay inside these ranges and needn't reach their ends.
Inputs may be any that keep to these rules, and one draw needn't show every extreme that they name: Each row of panel_order is a permutation of the 8 separators of that front.
All inputs are finite; a program needn't handle non-finite values.
Results may differ from the reference program's by a relative error of at most 0.025.
Values may be sent and summed in bfloat16 or wider, within the bound.
A program may use at most 128 MiB of HBM per device.

```python
import jax
import jax.numpy as jnp
from jax import lax

B = 128
R = 256
P_SIZE = 5
K_DEV = 32
SEP_DEV = 1
LEAVES = 1024
SEPS = 8
NSEP = 32
N_LEAF = 4
N_FRONT = 8


def touch_ends(values, stream_key, low, largest):
    longest = values.shape.index(max(values.shape))
    spots = []
    for shift in (0, 1):
        where = [jax.random.randint(jax.random.fold_in(stream_key, axis), (), 0, length) for axis, length in enumerate(values.shape)]
        where[longest] = (where[longest] + shift) % values.shape[longest]
        spots.append(tuple(where))
    return values.at[spots[0]].set(low).at[spots[1]].set(largest)


def block_scale(rng, shape, cuts, smallest, largest):
    gain = 1.0
    for dim, blocks in cuts:
        heights = jax.random.uniform(jax.random.fold_in(jax.random.fold_in(rng, 6), dim), (blocks,), jnp.float32, smallest / len(cuts), largest / len(cuts))
        gain = gain * jnp.repeat(jnp.exp(heights), shape[dim] // blocks).reshape((-1,) + (1,) * (len(shape) - 1 - dim))
    return gain


def scatter_about(stream_key, dims, width, bound, shards=(), kind=jnp.bfloat16):
    factor_of = block_scale(stream_key, dims, shards, -0.22, 0.18) if shards else 1.0
    entries = jax.random.normal(stream_key, dims, jnp.float32) * width * factor_of
    return jnp.minimum(jnp.maximum(entries, -bound), bound).astype(kind)


def setup_inputs(seed: int = 0) -> dict:
    key_of = jax.random.split(jax.random.key(seed), 9)
    return {
        "leaf_inverse": scatter_about(key_of[0], (LEAVES, B, B), B ** -0.5, 0.5, ((0, 32),)),
        "leaf_rhs": scatter_about(key_of[1], (LEAVES, B, R), 1.0, 6.0, ((0, 32),)),
        "off_blocks": scatter_about(key_of[2], (LEAVES, P_SIZE, B, B), (3 * B * K_DEV // SEP_DEV) ** -0.5, 0.0546875, ((0, 32),)),
        "block_rows": touch_ends(jax.random.randint(key_of[3], (LEAVES, P_SIZE), 0, 2 * SEPS), jax.random.fold_in(key_of[3], 1), 0, (2 * SEPS) - 1).astype(jnp.int32),
        "fill_count": touch_ends(jax.random.randint(key_of[4], (LEAVES,), 1, P_SIZE + 1), jax.random.fold_in(key_of[4], 1), 1, P_SIZE).astype(jnp.int32),
        "sep_rhs": scatter_about(key_of[5], (NSEP, B, R), 1.0, 6.0, ((0, 32),)),
        "panel_order": jax.vmap(lambda own: jax.random.permutation(own, SEPS))(jax.random.split(key_of[6], N_LEAF)).reshape((N_LEAF, SEPS)).astype(jnp.int32),
        "sep_inverse": scatter_about(key_of[7], (NSEP, B, SEPS * B), (SEPS * B) ** -0.5, 0.1875, ((0, 32),)),
    }


def forward_leaves(pieces):
    inverse_one, rhs_one = pieces
    return jnp.einsum('kab,kbr->kar', inverse_one.astype(jnp.float32), rhs_one.astype(jnp.float32)).astype(jnp.bfloat16)


def reference(leaf_inverse, leaf_rhs, off_blocks, block_rows, fill_count, sep_rhs, panel_order, sep_inverse):
    devices = N_LEAF * N_FRONT
    front_seps = SEP_DEV * N_FRONT
    inverse_dev = leaf_inverse.reshape(devices, K_DEV, B, B)
    rhs_dev = leaf_rhs.reshape(devices, K_DEV, B, R)
    off_dev = off_blocks.reshape(devices, K_DEV, P_SIZE, B, B)
    rows_dev = block_rows.reshape(devices, K_DEV, P_SIZE)
    fill_dev = fill_count.reshape(devices, K_DEV)
    forward = lax.map(forward_leaves, (inverse_dev, rhs_dev))
    indices = jnp.arange(devices, dtype=jnp.int32)
    bases = ((indices // N_FRONT) // 2) * 2 * front_seps
    slot_index = jnp.arange(P_SIZE, dtype=jnp.int32)

    def add_device(summed, pieces):
        off_one, forward_one, rows_one, fill_one, base_one = pieces
        product = jnp.einsum('kpab,kbr->kpar', off_one.astype(jnp.float32), forward_one.astype(jnp.float32))
        used_slots = slot_index[None, :] < fill_one[:, None]
        product = jnp.where(used_slots[:, :, None, None], product, jnp.zeros((), jnp.float32))
        target = (base_one + rows_one).reshape(-1).astype(jnp.int32)
        summed = summed.at[target].add(product.reshape(-1, B, R))
        return summed, None

    summed, _ = lax.scan(add_device, jnp.zeros((N_LEAF * front_seps, B, R), jnp.float32),
                         (off_dev, forward, rows_dev, fill_dev, bases))
    separator_in = (sep_rhs.astype(jnp.float32) - summed).astype(jnp.bfloat16)
    slot_rows = sep_inverse.reshape(N_LEAF, front_seps, B, front_seps * B)

    def to_natural(slot_block, order_row):
        return jnp.zeros_like(slot_block).at[order_row].set(slot_block)

    natural = jax.vmap(to_natural)(slot_rows, panel_order)

    def solve_front(pieces):
        matrix, rhs_group = pieces
        matrix = matrix.reshape(front_seps * B, front_seps * B)
        flat = rhs_group.reshape(front_seps * B, R)
        solved_forward = jnp.dot(matrix, flat, preferred_element_type=jnp.float32).astype(jnp.bfloat16)
        adjoint_out = jnp.dot(matrix.T, solved_forward, preferred_element_type=jnp.float32)
        return solved_forward, adjoint_out

    sep_fwd, sep_adj = lax.map(solve_front, (natural, separator_in.reshape(N_LEAF, front_seps, B, R)))
    sep_forward = sep_fwd.reshape(N_LEAF * front_seps, B, R)
    sep_solution = sep_adj.reshape(N_LEAF * front_seps, B, R)
    solved = sep_solution.astype(jnp.bfloat16)

    def back_device(pieces):
        inverse_one, off_one, forward_one, rows_one, fill_one, base_one = pieces
        picked = solved[(base_one + rows_one).astype(jnp.int32)]
        used_slots = slot_index[None, :] < fill_one[:, None]
        picked = jnp.where(used_slots[:, :, None, None], picked, jnp.zeros((), jnp.bfloat16))
        pulled = jnp.einsum('kpab,kpar->kbr', off_one.astype(jnp.float32), picked.astype(jnp.float32))
        backward = (forward_one.astype(jnp.float32) - pulled).astype(jnp.bfloat16)
        return jnp.einsum('kba,kbr->kar', inverse_one.astype(jnp.float32), backward.astype(jnp.float32)).astype(jnp.bfloat16)

    leaf_out = lax.map(back_device, (inverse_dev, off_dev, forward, rows_dev, fill_dev, bases))
    return leaf_out.reshape(devices * K_DEV, B, R), sep_forward, sep_solution
```

```python
import functools
import math

import jax
import jax.numpy as jnp
from jax import lax
from jax.experimental import pallas as pl
from jax.experimental.pallas import tpu as pltpu
from jax.sharding import PartitionSpec as P

MESH = pl.DeviceIdType.MESH
F32 = jnp.float32
BF16 = jnp.bfloat16
LEAF_STEP = 4
VMEM_BYTES = 56 * 1024 * 1024
FIRST_DIMS = (((0,), (0,)), ((), ()))


def leaf_forward(rows_ref, fill_ref, inverse_ref, rhs_ref, off_ref, forward_ref, partial_ref, acc):
    step = pl.program_id(0)
    seps = partial_ref.shape[0]
    slots, width = off_ref.shape[1], off_ref.shape[2]

    @pl.when(step == 0)
    def _():
        acc[...] = jnp.zeros_like(acc)

    for i in range(LEAF_STEP):
        leaf = step * LEAF_STEP + i
        forward = jnp.dot(inverse_ref[i], rhs_ref[i], preferred_element_type=F32).astype(BF16)
        forward_ref[i] = forward
        product = jnp.dot(
            off_ref[i].reshape(slots * width, width), forward, preferred_element_type=F32
        )
        for p in range(slots):
            target = jnp.where(p < fill_ref[leaf], rows_ref[leaf, p], seps)
            acc[target] += product[p * width : (p + 1) * width]

    @pl.when(step == pl.num_programs(0) - 1)
    def _():
        partial_ref[...] = acc[:seps].astype(BF16)


def leaf_backward(rows_ref, fill_ref, field_ref, inverse_ref, off_ref, forward_ref, out_ref):
    step = pl.program_id(0)
    slots, width = off_ref.shape[1], off_ref.shape[2]
    for i in range(LEAF_STEP):
        leaf = step * LEAF_STEP + i
        picked = []
        for p in range(slots):
            block = field_ref[rows_ref[leaf, p]]
            picked.append(jnp.where(p < fill_ref[leaf], block, jnp.zeros_like(block)))
        pulled = lax.dot_general(
            off_ref[i].reshape(slots * width, width),
            jnp.concatenate(picked, axis=0),
            FIRST_DIMS,
            preferred_element_type=F32,
        )
        backward = (forward_ref[i].astype(F32) - pulled).astype(BF16)
        out_ref[i] = lax.dot_general(
            inverse_ref[i], backward, FIRST_DIMS, preferred_element_type=F32
        ).astype(BF16)


def separators(
    zs, xs, order_ref, partial_ref, rhs_ref, panel_ref, column_ref,
    field_ref, forward_ref, solution_ref,
    from_core, to_x, from_x, to_z, from_z, gathered_in, gathered_fwd,
    core_send, core_recv, x_send, x_recv, z_send, z_recv,
    in_sems, fwd_sems, sol_sems, sib_send, sib_recv,
):
    fronts = zs * xs
    width = rhs_ref.shape[1]
    leaf, me = lax.axis_index("leaf"), lax.axis_index("front")
    half = lax.rem(leaf, 2)
    z, x = me // xs, lax.rem(me, xs)
    sibling = (leaf + 1 - 2 * half, me)

    def at(zz, xx):
        return (leaf, zz * xs + xx)

    other_z = [lax.rem(z + k, zs) for k in range(1, zs)]
    other_x = [lax.rem(x + k, xs) for k in range(1, xs)]

    barrier = pltpu.get_barrier_semaphore()
    peers = [at(zz, x) for zz in other_z] + [at(z, xx) for xx in other_x] + [sibling]
    for peer in peers:
        pl.semaphore_signal(barrier, inc=1, device_id=peer, device_id_type=MESH)
    pl.semaphore_wait(barrier, len(peers))

    sent = []

    def remote(src, dst, send, recv, device):
        return pltpu.make_async_remote_copy(
            src_ref=src, dst_ref=dst, send_sem=send, recv_sem=recv,
            device_id=device, device_id_type=MESH,
        )

    def push(src, dst, send, recv, device):
        copy = remote(src, dst, send, recv, device)
        copy.start()
        sent.append(copy)

    def arrived(dst, recv):
        remote(dst, dst, recv, recv, sibling).wait_recv()

    order = other_z + [z]
    for zz in order:
        push(
            partial_ref.at[pl.ds((1 - half) * fronts + zz * xs, xs)],
            from_core.at[pl.ds(zz * xs, xs)],
            core_send.at[zz], core_recv.at[zz], sibling,
        )
    for zz in order:
        arrived(from_core.at[pl.ds(zz * xs, xs)], core_recv.at[zz])
        for xx in other_x:
            f = zz * xs + xx
            to_x[f] = (
                partial_ref[half * fronts + f].astype(F32) + from_core[f].astype(F32)
            ).astype(BF16)
            push(
                to_x.at[f], from_x.at[zz * xs + x], x_send.at[f], x_recv.at[zz * xs + x], at(z, xx)
            )
    total = None
    for zz in order:
        f = zz * xs + x
        total = partial_ref[half * fronts + f].astype(F32) + from_core[f].astype(F32)
        for xx in other_x:
            arrived(from_x.at[zz * xs + xx], x_recv.at[zz * xs + xx])
            total += from_x[zz * xs + xx].astype(F32)
        if zz is not z:
            to_z[zz] = total.astype(BF16)
            push(to_z.at[zz], from_z.at[z], z_send.at[zz], z_recv.at[z], at(zz, x))
    for zz in other_z:
        arrived(from_z.at[zz], z_recv.at[zz])
        total += from_z[zz].astype(F32)

    def gather(buffer, base, sems, use):
        z_out, z_in, x_out, x_in = sems
        own = buffer.at[base + me]
        for xx in other_x:
            push(own, own, x_out.at[z * xs + xx], x_in.at[me], at(z, xx))
        for zz in other_z:
            push(own, own, z_out.at[zz], z_in.at[z], at(zz, x))
        use(me)
        for zz in other_z:
            f = zz * xs + x
            block = buffer.at[base + f]
            arrived(block, z_in.at[zz])
            for xx in other_x:
                push(block, block, x_out.at[zz * xs + xx], x_in.at[f], at(z, xx))
            use(f)
        for zz in [z] + other_z:
            for xx in other_x:
                f = zz * xs + xx
                arrived(buffer.at[base + f], x_in.at[f])
                use(f)

    result = []

    def add(matrix_of, vectors):
        def use(f):
            term = jnp.dot(matrix_of(f), vectors[f], preferred_element_type=F32)
            result[:] = [result[0] + term] if result else [term]

        return use

    gathered_in[me] = (rhs_ref[0].astype(F32) - total).astype(BF16)
    gather(gathered_in, 0, in_sems, add(lambda f: panel_ref[f], gathered_in))
    gathered_fwd[me] = result.pop().astype(BF16)
    gather(gathered_fwd, 0, fwd_sems, add(lambda f: column_ref[f], gathered_fwd))
    solved = result.pop()
    base = half * fronts
    field_ref[base + me] = solved.astype(BF16)

    def to_sibling(f):
        block = field_ref.at[base + f]
        push(block, block, sib_send.at[f], sib_recv.at[f], sibling)

    gather(field_ref, base, sol_sems, to_sibling)
    solution_ref[0] = solved
    slot = jnp.int32(0)
    for p in range(fronts):
        slot = jnp.where(order_ref[0, p] == me, p, slot)
    forward_ref[0] = gathered_fwd[slot]
    for zz in [z] + other_z:
        for xx in [x] + other_x:
            f = zz * xs + xx
            arrived(field_ref.at[(1 - half) * fronts + f], sib_recv.at[f])
    for copy in sent:
        copy.wait_send()


def on_device(
    leaf_inverse, leaf_rhs, off_blocks, block_rows, fill_count, sep_rhs, panel_order, sep_inverse
):
    leaves, width = leaf_inverse.shape[:2]
    probes = leaf_rhs.shape[2]
    slots = off_blocks.shape[1]
    fronts = lax.axis_size("front")
    xs = math.isqrt(fronts // 2)
    zs = fronts // xs
    steps = leaves // LEAF_STEP
    block = (width, probes)
    panel = sep_inverse.reshape(width, fronts, width)
    columns = lax.all_to_all(jnp.transpose(panel, (1, 2, 0)), "front", 0, 0, tiled=True)
    panel = jnp.transpose(panel, (1, 0, 2))

    smem = pl.BlockSpec(memory_space=pltpu.SMEM)
    vmem = pl.BlockSpec(memory_space=pltpu.VMEM)
    inverse_spec = pl.BlockSpec((LEAF_STEP, width, width), lambda i: (i, 0, 0))
    vector_spec = pl.BlockSpec((LEAF_STEP,) + block, lambda i: (i, 0, 0))
    off_spec = pl.BlockSpec((LEAF_STEP, slots, width, width), lambda i: (i, 0, 0, 0))
    flops = 2 * leaves * (slots + 1) * width * width * probes
    moved = 2 * leaves * width * (width * (slots + 1) + 2 * probes)
    cost = pl.CostEstimate(flops=flops, bytes_accessed=moved, transcendentals=0)

    forward, partial = pl.pallas_call(
        leaf_forward,
        grid=(steps,),
        out_shape=(
            jax.ShapeDtypeStruct((leaves,) + block, BF16),
            jax.ShapeDtypeStruct((2 * fronts,) + block, BF16),
        ),
        in_specs=[smem, smem, inverse_spec, vector_spec, off_spec],
        out_specs=(vector_spec, pl.BlockSpec((2 * fronts,) + block, lambda i: (0, 0, 0))),
        scratch_shapes=[pltpu.VMEM((2 * fronts + 1,) + block, F32)],
        compiler_params=pltpu.CompilerParams(vmem_limit_bytes=VMEM_BYTES),
        cost_estimate=cost,
        name="leaf_forward",
    )(block_rows, fill_count, leaf_inverse, leaf_rhs, off_blocks)

    dma = pltpu.SemaphoreType.DMA
    gather_sems = [dma((zs,)), dma((zs,)), dma((fronts,)), dma((fronts,))]

    def kernel(*refs):
        head, sems = refs[:15], list(refs[15:])
        groups = [tuple(sems[6 + 4 * k : 10 + 4 * k]) for k in range(3)]
        separators(zs, xs, *head, *sems[:6], *groups, *sems[18:])

    field, sep_forward, sep_solution = pl.pallas_call(
        kernel,
        out_shape=(
            jax.ShapeDtypeStruct((2 * fronts,) + block, BF16),
            jax.ShapeDtypeStruct((1,) + block, BF16),
            jax.ShapeDtypeStruct((1,) + block, F32),
        ),
        in_specs=[smem, vmem, vmem, vmem, vmem],
        out_specs=(vmem, vmem, vmem),
        scratch_shapes=[
            pltpu.VMEM((fronts,) + block, BF16),
            pltpu.VMEM((fronts,) + block, BF16),
            pltpu.VMEM((fronts,) + block, BF16),
            pltpu.VMEM((zs,) + block, BF16),
            pltpu.VMEM((zs,) + block, BF16),
            pltpu.VMEM((fronts,) + block, BF16),
            pltpu.VMEM((fronts,) + block, BF16),
            dma((zs,)), dma((zs,)), dma((fronts,)), dma((fronts,)), dma((zs,)), dma((zs,)),
            *gather_sems, *gather_sems, *gather_sems,
            dma((fronts,)), dma((fronts,)),
        ],
        compiler_params=pltpu.CompilerParams(
            collective_id=0, has_side_effects=True, vmem_limit_bytes=VMEM_BYTES
        ),
        cost_estimate=pl.CostEstimate(
            flops=4 * fronts * width * width * probes,
            bytes_accessed=8 * fronts * width * probes,
            transcendentals=0,
        ),
        name="separators",
    )(panel_order, partial, sep_rhs, panel, columns)

    leaf_solution = pl.pallas_call(
        leaf_backward,
        grid=(steps,),
        out_shape=jax.ShapeDtypeStruct((leaves,) + block, BF16),
        in_specs=[
            smem, smem, pl.BlockSpec((2 * fronts,) + block, lambda i: (0, 0, 0)),
            inverse_spec, off_spec, vector_spec,
        ],
        out_specs=vector_spec,
        compiler_params=pltpu.CompilerParams(vmem_limit_bytes=VMEM_BYTES),
        cost_estimate=cost,
        name="leaf_backward",
    )(block_rows, fill_count, field, leaf_inverse, off_blocks, forward)
    return (leaf_solution, sep_forward, sep_solution)


def solution(mesh):
    placed = (
        P(("leaf", "front"), None, None),
        P(("leaf", "front"), None, None),
        P(("leaf", "front"), None, None, None),
        P(("leaf", "front"), None),
        P(("leaf", "front")),
        P(("leaf", "front"), None, None),
        P("leaf", None),
        P(("leaf", "front"), None, None),
    )
    return jax.shard_map(
        on_device,
        mesh=mesh,
        in_specs=placed,
        out_specs=(
            P(("leaf", "front"), None, None),
            P(("leaf", "front"), None, None),
            P(("leaf", "front"), None, None),
        ),
        check_vma=False,
    )
```

```python
import jax
import jax.numpy as jnp
from jax import lax
from jax.experimental import pallas as pl
from jax.experimental.pallas import tpu as pltpu
from jax.sharding import PartitionSpec as P

MESH = pl.DeviceIdType.MESH
F32 = jnp.float32
BF16 = jnp.bfloat16
LEAF_STEP = 4
VMEM_BYTES = 56 * 1024 * 1024
FIRST_DIMS = (((0,), (0,)), ((), ()))


def leaf_forward(rows_ref, fill_ref, inverse_ref, rhs_ref, off_ref, forward_ref, partial_ref, acc):
    step = pl.program_id(0)
    chunks, seps, _, lanes = partial_ref.shape
    slots, width = off_ref.shape[1], off_ref.shape[2]

    @pl.when(step == 0)
    def _():
        acc[...] = jnp.zeros_like(acc)

    for i in range(LEAF_STEP):
        leaf = step * LEAF_STEP + i
        forward = jnp.dot(inverse_ref[i], rhs_ref[i], preferred_element_type=F32).astype(BF16)
        forward_ref[i] = forward
        product = jnp.dot(
            off_ref[i].reshape(slots * width, width), forward, preferred_element_type=F32
        )
        for p in range(slots):
            target = jnp.where(p < fill_ref[leaf], rows_ref[p, leaf], seps)
            acc[target] += product[p * width : (p + 1) * width]

    @pl.when(step == pl.num_programs(0) - 1)
    def _():
        for c in range(chunks):
            partial_ref[c] = acc[:seps, :, c * lanes : (c + 1) * lanes].astype(BF16)


def leaf_backward(
    rows_ref, fill_ref, field_ref, inverse_ref, off_ref, forward_ref, sep_fwd_ref, sep_sol_ref,
    out_ref, sep_fwd_out, sep_sol_out,
):
    step = pl.program_id(0)
    slots, width = off_ref.shape[1], off_ref.shape[2]

    @pl.when(step == 0)
    def _():
        sep_fwd_out[...] = sep_fwd_ref[...]
        sep_sol_out[...] = sep_sol_ref[...]

    for i in range(LEAF_STEP):
        leaf = step * LEAF_STEP + i
        picked = []
        for p in range(slots):
            row = rows_ref[p, leaf]
            block = jnp.concatenate([field_ref[c, row] for c in range(field_ref.shape[0])], axis=1)
            picked.append(jnp.where(p < fill_ref[leaf], block, jnp.zeros_like(block)))
        pulled = lax.dot_general(
            off_ref[i].reshape(slots * width, width),
            jnp.concatenate(picked, axis=0),
            FIRST_DIMS,
            preferred_element_type=F32,
        )
        backward = (forward_ref[i].astype(F32) - pulled).astype(BF16)
        out_ref[i] = lax.dot_general(
            inverse_ref[i], backward, FIRST_DIMS, preferred_element_type=F32
        ).astype(BF16)


def separators(
    order_ref, partial_ref, rhs_ref, panel_ref, peer_panel_ref,
    field_ref, forward_ref, solution_ref,
    from_core, to_x, from_x, to_z, from_z, gathered_in, to_adjoint, from_adjoint, gathered_fwd,
    to_peer, from_peer, panel_t,
    core_send, core_recv, x_send, x_recv, z_send, z_recv, in_send, in_recv, adj_send, adj_recv,
    fwd_send, fwd_recv, sol_send, sol_recv, sol_x_send, sol_x_recv, sib_send, sib_recv,
    peer_send, peer_recv,
):
    chunks, seps, width, lanes = partial_ref.shape
    fronts = seps // 2
    lines = fronts // chunks
    leaf, me = lax.axis_index("leaf"), lax.axis_index("front")
    half = lax.rem(leaf, 2)
    line, part = me // chunks, lax.rem(me, chunks)
    base, far_base = half * fronts, (1 - half) * fronts
    sibling = (leaf + 1 - 2 * half, me)
    others = [lax.rem(line + k, lines) for k in range(1, lines)]
    parts = [lax.rem(part + k, chunks) for k in range(1, chunks)]
    order = others + [line]

    def along(ll):
        return (leaf, ll * chunks + part)

    def across(pp):
        return (leaf, line * chunks + pp)

    def group(ll, start=0):
        return pl.ds(start + ll * chunks, chunks)

    barrier = pltpu.get_barrier_semaphore()
    peers = [along(ll) for ll in others] + [across(pp) for pp in parts] + [sibling]
    for peer in peers:
        pl.semaphore_signal(barrier, inc=1, device_id=peer, device_id_type=MESH)
    pl.semaphore_wait(barrier, len(peers))

    sent = []

    def remote(src, dst, send, recv, device):
        return pltpu.make_async_remote_copy(
            src_ref=src, dst_ref=dst, send_sem=send, recv_sem=recv,
            device_id=device, device_id_type=MESH,
        )

    def push(src, dst, send, recv, device):
        copy = remote(src, dst, send, recv, device)
        copy.start()
        sent.append(copy)

    def arrived(dst, recv):
        remote(dst, dst, recv, recv, sibling).wait_recv()

    rhs = [rhs_ref[0, :, c * lanes : (c + 1) * lanes].astype(F32) for c in range(chunks)]

    def rhs_of(pp):
        value = rhs[0]
        for c in range(1, chunks):
            value = jnp.where(pp == c, rhs[c], value)
        return value

    for pp in parts + [part]:
        for ll in order:
            push(
                partial_ref.at[pp, group(ll, far_base)], from_core.at[pp, group(ll)],
                core_send.at[pp, ll], core_recv.at[pp, ll], sibling,
            )

    def pair_sum(pp, f):
        return partial_ref[pp, base + f].astype(F32) + from_core[pp, f].astype(F32)

    for pp in parts:
        for ll in order:
            arrived(from_core.at[pp, group(ll)], core_recv.at[pp, ll])
            for k in range(chunks):
                f = ll * chunks + k
                value = pair_sum(pp, f)
                if ll is line:
                    value = jnp.where(part == k, value - rhs_of(pp), value)
                to_x[pp, f] = value.astype(BF16)
            push(
                to_x.at[pp, group(ll)], from_x.at[part, group(ll)],
                x_send.at[pp, ll], x_recv.at[part, ll], across(pp),
            )
    totals = []
    for ll in order:
        arrived(from_core.at[part, group(ll)], core_recv.at[part, ll])
        for pp in parts:
            arrived(from_x.at[pp, group(ll)], x_recv.at[pp, ll])
        for k in range(chunks):
            f = ll * chunks + k
            value = pair_sum(part, f)
            for pp in parts:
                value += from_x[pp, f].astype(F32)
            if ll is line:
                totals.append(jnp.where(part == k, value - rhs_of(part), value))
            else:
                to_z[f] = value.astype(BF16)
        if ll is not line:
            push(to_z.at[group(ll)], from_z.at[group(line)], z_send.at[ll], z_recv.at[line], along(ll))
    for ll in others:
        arrived(from_z.at[group(ll)], z_recv.at[ll])
        for k in range(chunks):
            totals[k] += from_z[ll * chunks + k].astype(F32)

    for k in range(chunks):
        gathered_in[line * chunks + k] = (-totals[k]).astype(BF16)
    mine = group(line)
    for ll in others:
        push(gathered_in.at[mine], gathered_in.at[mine], in_send.at[ll], in_recv.at[line], along(ll))

    panels = [panel_ref] + [peer_panel_ref.at[k] for k in range(chunks - 1)]
    for f in range(fronts):
        for k, panel in enumerate(panels):
            panel_t[f * width : (f + 1) * width, k * width : (k + 1) * width] = panel[
                :, f * width : (f + 1) * width
            ].T

    forward = [jnp.zeros((width, lanes), F32)] * chunks
    for ll in [line] + others:
        if ll is not line:
            arrived(gathered_in.at[group(ll)], in_recv.at[ll])
        vectors = gathered_in[group(ll)].reshape(chunks * width, lanes)
        columns = pl.ds(pl.multiple_of(ll * chunks * width, chunks * width), chunks * width)
        for k, panel in enumerate(panels):
            forward[k] += jnp.dot(panel[:, columns], vectors, preferred_element_type=F32)
    forward = [value.astype(BF16) for value in forward]
    stacked = jnp.concatenate(forward, axis=0)
    for k in range(chunks):
        gathered_fwd[line * chunks + lax.rem(part + k, chunks)] = forward[k]

    solved = None
    for ll in order:
        rows = pl.ds(pl.multiple_of(ll * chunks * width, chunks * width), chunks * width)
        term = jnp.dot(panel_t[rows, :], stacked, preferred_element_type=F32)
        if ll is line:
            solved = term
        else:
            to_adjoint[group(ll)] = term.astype(BF16).reshape(chunks, width, lanes)
            push(
                to_adjoint.at[group(ll)], from_adjoint.at[mine],
                adj_send.at[ll], adj_recv.at[line], along(ll),
            )
    for ll in others:
        arrived(from_adjoint.at[group(ll)], adj_recv.at[ll])
        solved += from_adjoint[group(ll)].reshape(chunks * width, lanes).astype(F32)

    def share(pp, ll):
        block = field_ref.at[pp, group(ll, base)]
        push(block, block, sib_send.at[pp, ll], sib_recv.at[pp, ll], sibling)

    def share_across(ll):
        block = field_ref.at[part, group(ll, base)]
        for pp in parts:
            push(block, block, sol_x_send.at[pp, ll], sol_x_recv.at[part, ll], across(pp))

    field_ref[part, group(line, base)] = solved.astype(BF16).reshape(chunks, width, lanes)
    own = field_ref.at[part, group(line, base)]
    for ll in others:
        push(own, own, sol_send.at[ll], sol_recv.at[line], along(ll))
    share_across(line)
    share(part, line)
    for ll in others:
        push(
            gathered_fwd.at[mine], gathered_fwd.at[mine],
            fwd_send.at[ll], fwd_recv.at[line], along(ll),
        )
    for ll in others:
        arrived(field_ref.at[part, group(ll, base)], sol_recv.at[ll])
        share_across(ll)
        share(part, ll)
    for ll in [line] + others:
        for pp in parts:
            arrived(field_ref.at[pp, group(ll, base)], sol_x_recv.at[pp, ll])
            share(pp, ll)
    for c in range(chunks):
        solution_ref[0, :, c * lanes : (c + 1) * lanes] = field_ref[c, base + me].astype(F32)

    for ll in others:
        arrived(gathered_fwd.at[group(ll)], fwd_recv.at[ll])

    def forward_of(sep):
        slot = jnp.int32(0)
        for p in range(fronts):
            slot = jnp.where(order_ref[0, p] == sep, p, slot)
        return gathered_fwd[slot]

    from_peer[part] = forward_of(me)
    for pp in parts:
        to_peer[pp] = forward_of(line * chunks + pp)
        push(to_peer.at[pp], from_peer.at[part], peer_send.at[pp], peer_recv.at[part], across(pp))
    for pp in parts + [part]:
        for ll in [line] + others:
            arrived(field_ref.at[pp, group(ll, far_base)], sib_recv.at[pp, ll])
    for pp in parts:
        arrived(from_peer.at[pp], peer_recv.at[pp])
    for c in range(chunks):
        forward_ref[0, :, c * lanes : (c + 1) * lanes] = from_peer[c]
    for copy in sent:
        copy.wait_send()


def on_device(
    leaf_inverse, leaf_rhs, off_blocks, block_rows, fill_count, sep_rhs, panel_order, sep_inverse
):
    leaves, width = leaf_inverse.shape[:2]
    probes = leaf_rhs.shape[2]
    slots = off_blocks.shape[1]
    fronts = lax.axis_size("front")
    steps = leaves // LEAF_STEP
    block = (width, probes)
    lanes = 128
    chunks = probes // lanes
    piece = (width, lanes)
    lines = fronts // chunks
    rows = block_rows.T
    panel = sep_inverse.reshape(width, fronts * width)
    peer_panels = jnp.stack(
        [
            lax.ppermute(
                panel,
                "front",
                [(i // chunks * chunks + (i + k) % chunks, i) for i in range(fronts)],
            )
            for k in range(1, chunks)
        ]
    )

    smem = pl.BlockSpec(memory_space=pltpu.SMEM)
    vmem = pl.BlockSpec(memory_space=pltpu.VMEM)
    inverse_spec = pl.BlockSpec((LEAF_STEP, width, width), lambda i: (i, 0, 0))
    vector_spec = pl.BlockSpec((LEAF_STEP,) + block, lambda i: (i, 0, 0))
    off_spec = pl.BlockSpec((LEAF_STEP, slots, width, width), lambda i: (i, 0, 0, 0))
    field_spec = pl.BlockSpec((chunks, 2 * fronts) + piece, lambda i: (0, 0, 0, 0))
    one_spec = pl.BlockSpec((1,) + block, lambda i: (0, 0, 0))
    flops = 2 * leaves * (slots + 1) * width * width * probes
    moved = 2 * leaves * width * (width * (slots + 1) + 2 * probes)
    cost = pl.CostEstimate(flops=flops, bytes_accessed=moved, transcendentals=0)

    forward, partial = pl.pallas_call(
        leaf_forward,
        grid=(steps,),
        out_shape=(
            jax.ShapeDtypeStruct((leaves,) + block, BF16),
            jax.ShapeDtypeStruct((chunks, 2 * fronts) + piece, BF16),
        ),
        in_specs=[smem, smem, inverse_spec, vector_spec, off_spec],
        out_specs=(vector_spec, field_spec),
        scratch_shapes=[pltpu.VMEM((2 * fronts + 1,) + block, F32)],
        compiler_params=pltpu.CompilerParams(vmem_limit_bytes=VMEM_BYTES),
        cost_estimate=cost,
        name="leaf_forward",
    )(rows, fill_count, leaf_inverse, leaf_rhs, off_blocks)

    dma = pltpu.SemaphoreType.DMA
    by_line, by_both = dma((lines,)), dma((chunks, lines))
    whole = pltpu.VMEM((chunks, fronts) + piece, BF16)
    part = pltpu.VMEM((fronts,) + piece, BF16)
    small = pltpu.VMEM((chunks,) + piece, BF16)

    field, sep_forward, sep_solution = pl.pallas_call(
        separators,
        out_shape=(
            jax.ShapeDtypeStruct((chunks, 2 * fronts) + piece, BF16),
            jax.ShapeDtypeStruct((1,) + block, BF16),
            jax.ShapeDtypeStruct((1,) + block, F32),
        ),
        in_specs=[smem, vmem, vmem, vmem, vmem],
        out_specs=(vmem, vmem, vmem),
        scratch_shapes=[
            whole, whole, whole, part, part, part, part, part, part, small, small,
            pltpu.VMEM((fronts * width, chunks * width), BF16),
            by_both, by_both, by_both, by_both, by_line, by_line, by_line, by_line,
            by_line, by_line, by_line, by_line, by_line, by_line, by_both, by_both,
            by_both, by_both, dma((chunks,)), dma((chunks,)),
        ],
        compiler_params=pltpu.CompilerParams(
            collective_id=0, has_side_effects=True, vmem_limit_bytes=VMEM_BYTES
        ),
        cost_estimate=pl.CostEstimate(
            flops=4 * fronts * width * width * probes,
            bytes_accessed=8 * fronts * width * probes,
            transcendentals=0,
        ),
        name="separators",
    )(panel_order, partial, sep_rhs, panel, peer_panels)

    return pl.pallas_call(
        leaf_backward,
        grid=(steps,),
        out_shape=(
            jax.ShapeDtypeStruct((leaves,) + block, BF16),
            jax.ShapeDtypeStruct((1,) + block, BF16),
            jax.ShapeDtypeStruct((1,) + block, F32),
        ),
        in_specs=[
            smem, smem, field_spec, inverse_spec, off_spec, vector_spec, one_spec, one_spec,
        ],
        out_specs=(vector_spec, one_spec, one_spec),
        compiler_params=pltpu.CompilerParams(vmem_limit_bytes=VMEM_BYTES),
        cost_estimate=cost,
        name="leaf_backward",
    )(rows, fill_count, field, leaf_inverse, off_blocks, forward, sep_forward, sep_solution)


def solution(mesh):
    placed = (
        P(("leaf", "front"), None, None),
        P(("leaf", "front"), None, None),
        P(("leaf", "front"), None, None, None),
        P(("leaf", "front"), None),
        P(("leaf", "front")),
        P(("leaf", "front"), None, None),
        P("leaf", None),
        P(("leaf", "front"), None, None),
    )
    return jax.shard_map(
        on_device,
        mesh=mesh,
        in_specs=placed,
        out_specs=(
            P(("leaf", "front"), None, None),
            P(("leaf", "front"), None, None),
            P(("leaf", "front"), None, None),
        ),
        check_vma=False,
    )
```

```python
import jax
import jax.numpy as jnp
from jax import lax
from jax.experimental import pallas as pl
from jax.experimental.pallas import tpu as pltpu
from jax.sharding import PartitionSpec as P

MESH = pl.DeviceIdType.MESH
F32 = jnp.float32
BF16 = jnp.bfloat16
LEAF_STEP = 8
VMEM_BYTES = 56 * 1024 * 1024


def leaf_forward(
    rows_ref, fill_ref, inverse_ref, rhs_ref, off_ref, forward_ref, turned_ref, partial_ref, *accs
):
    step = pl.program_id(0)
    chunks, seps, _, lanes = partial_ref.shape
    slots, width = off_ref.shape[1], off_ref.shape[2]
    bands = len(accs) // chunks
    band = width // bands

    @pl.when(step == 0)
    def _():
        for acc in accs:
            acc[...] = jnp.zeros_like(acc)

    for i in range(LEAF_STEP):
        leaf = step * LEAF_STEP + i
        forward = jnp.dot(inverse_ref[i], rhs_ref[i], preferred_element_type=F32).astype(BF16)
        forward_ref[i] = forward
        stacked = off_ref[i].reshape(slots * width, width)
        product = jnp.dot(stacked, forward, preferred_element_type=F32)
        turned_ref[i, :, : slots * width] = stacked.T
        turned_ref[i, :, slots * width :] = inverse_ref[i].T
        for p in range(slots):
            target = jnp.where(p < fill_ref[leaf], rows_ref[p, leaf], seps)
            for k, acc in enumerate(accs):
                c, top = k % chunks, p * width + k // chunks * band
                acc[target] += product[top : top + band, c * lanes : (c + 1) * lanes]

    @pl.when(step == pl.num_programs(0) - 1)
    def _():
        for k, acc in enumerate(accs):
            top = k // chunks * band
            partial_ref[k % chunks, :, top : top + band, :] = acc[:seps].astype(BF16)


def leaf_backward(
    rows_ref, fill_ref, field_ref, turned_ref, forward_ref, sep_fwd_ref, sep_sol_ref,
    out_ref, sep_fwd_out, sep_sol_out,
):
    step = pl.program_id(0)
    slots, width = rows_ref.shape[0], turned_ref.shape[1]

    @pl.when(step == 0)
    def _():
        sep_fwd_out[...] = sep_fwd_ref[...]
        sep_sol_out[...] = sep_sol_ref[...]

    for i in range(LEAF_STEP):
        leaf = step * LEAF_STEP + i
        picked = []
        for p in range(slots):
            row = rows_ref[p, leaf]
            block = jnp.concatenate([field_ref[c, row] for c in range(field_ref.shape[0])], axis=1)
            picked.append(jnp.where(p < fill_ref[leaf], block, jnp.zeros_like(block)))
        pulled = jnp.dot(
            turned_ref[i, :, : slots * width],
            jnp.concatenate(picked, axis=0),
            preferred_element_type=F32,
        )
        backward = (forward_ref[i].astype(F32) - pulled).astype(BF16)
        out_ref[i] = jnp.dot(
            turned_ref[i, :, slots * width :], backward, preferred_element_type=F32
        ).astype(BF16)


def separators(
    order_ref, partial_ref, rhs_ref, panel_ref,
    field_ref, forward_ref, solution_ref,
    from_core, to_x, from_x, to_z, from_z, gathered_in, to_adjoint, from_adjoint, gathered_fwd,
    to_peer, from_peer, panel_t, peer_panel,
    core_send, core_recv, x_send, x_recv, z_send, z_recv, in_send, in_recv, adj_send, adj_recv,
    fwd_send, fwd_recv, sol_send, sol_recv, sol_x_send, sol_x_recv, sib_send, sib_recv,
    peer_send, peer_recv, panel_send, panel_recv,
):
    chunks, seps, width, lanes = partial_ref.shape
    fronts = seps // 2
    lines = fronts // chunks
    leaf, me = lax.axis_index("leaf"), lax.axis_index("front")
    half = lax.rem(leaf, 2)
    line, part = me // chunks, lax.rem(me, chunks)
    base, far_base = half * fronts, (1 - half) * fronts
    sibling = (leaf + 1 - 2 * half, me)
    others = [lax.rem(line + k, lines) for k in range(1, lines)]
    parts = [lax.rem(part + k, chunks) for k in range(1, chunks)]
    order = others + [line]

    def along(ll):
        return (leaf, ll * chunks + part)

    def across(pp):
        return (leaf, line * chunks + pp)

    def group(ll, start=0):
        return pl.ds(start + ll * chunks, chunks)

    barrier = pltpu.get_barrier_semaphore()
    peers = [along(ll) for ll in others] + [across(pp) for pp in parts] + [sibling]
    for peer in peers:
        pl.semaphore_signal(barrier, inc=1, device_id=peer, device_id_type=MESH)
    pl.semaphore_wait(barrier, len(peers))

    sent = []

    def remote(src, dst, send, recv, device):
        return pltpu.make_async_remote_copy(
            src_ref=src, dst_ref=dst, send_sem=send, recv_sem=recv,
            device_id=device, device_id_type=MESH,
        )

    def push(src, dst, send, recv, device):
        copy = remote(src, dst, send, recv, device)
        copy.start()
        sent.append(copy)

    def arrived(dst, recv):
        remote(dst, dst, recv, recv, sibling).wait_recv()

    rhs = [rhs_ref[0, :, c * lanes : (c + 1) * lanes].astype(F32) for c in range(chunks)]

    def rhs_of(pp):
        value = rhs[0]
        for c in range(1, chunks):
            value = jnp.where(pp == c, rhs[c], value)
        return value

    for pp in parts + [part]:
        for ll in order:
            push(
                partial_ref.at[pp, group(ll, far_base)], from_core.at[pp, group(ll)],
                core_send.at[pp, ll], core_recv.at[pp, ll], sibling,
            )

    def pair_sum(pp, f):
        return partial_ref[pp, base + f].astype(F32) + from_core[pp, f].astype(F32)

    for pp in parts:
        for ll in order:
            arrived(from_core.at[pp, group(ll)], core_recv.at[pp, ll])
            for k in range(chunks):
                f = ll * chunks + k
                value = pair_sum(pp, f)
                if ll is line:
                    value = jnp.where(part == k, value - rhs_of(pp), value)
                to_x[pp, f] = value.astype(BF16)
            push(
                to_x.at[pp, group(ll)], from_x.at[part, group(ll)],
                x_send.at[pp, ll], x_recv.at[part, ll], across(pp),
            )
    for pp in parts:
        push(panel_ref, peer_panel.at[part], panel_send.at[pp], panel_recv.at[part], across(pp))
    totals = []
    for ll in order:
        arrived(from_core.at[part, group(ll)], core_recv.at[part, ll])
        for pp in parts:
            arrived(from_x.at[pp, group(ll)], x_recv.at[pp, ll])
        for k in range(chunks):
            f = ll * chunks + k
            value = pair_sum(part, f)
            for pp in parts:
                value += from_x[pp, f].astype(F32)
            if ll is line:
                totals.append(jnp.where(part == k, value - rhs_of(part), value))
            else:
                to_z[f] = value.astype(BF16)
        if ll is not line:
            push(to_z.at[group(ll)], from_z.at[group(line)], z_send.at[ll], z_recv.at[line], along(ll))
    for ll in others:
        arrived(from_z.at[group(ll)], z_recv.at[ll])
        for k in range(chunks):
            totals[k] += from_z[ll * chunks + k].astype(F32)

    for k in range(chunks):
        gathered_in[line * chunks + k] = (-totals[k]).astype(BF16)
    mine = group(line)
    for ll in others:
        push(gathered_in.at[mine], gathered_in.at[mine], in_send.at[ll], in_recv.at[line], along(ll))

    for pp in parts:
        arrived(peer_panel.at[pp], panel_recv.at[pp])
    panels = [panel_ref] + [peer_panel.at[pp] for pp in parts]
    for f in range(fronts):
        for k, panel in enumerate(panels):
            panel_t[f * width : (f + 1) * width, k * width : (k + 1) * width] = panel[
                :, f * width : (f + 1) * width
            ].T

    forward = [jnp.zeros((width, lanes), F32)] * chunks
    for ll in [line] + others:
        if ll is not line:
            arrived(gathered_in.at[group(ll)], in_recv.at[ll])
        vectors = gathered_in[group(ll)].reshape(chunks * width, lanes)
        columns = pl.ds(pl.multiple_of(ll * chunks * width, chunks * width), chunks * width)
        for k, panel in enumerate(panels):
            forward[k] += jnp.dot(panel[:, columns], vectors, preferred_element_type=F32)
    forward = [value.astype(BF16) for value in forward]
    stacked = jnp.concatenate(forward, axis=0)
    for k in range(chunks):
        gathered_fwd[line * chunks + lax.rem(part + k, chunks)] = forward[k]

    solved = None
    for ll in order:
        rows = pl.ds(pl.multiple_of(ll * chunks * width, chunks * width), chunks * width)
        term = jnp.dot(panel_t[rows, :], stacked, preferred_element_type=F32)
        if ll is line:
            solved = term
        else:
            to_adjoint[group(ll)] = term.astype(BF16).reshape(chunks, width, lanes)
            push(
                to_adjoint.at[group(ll)], from_adjoint.at[mine],
                adj_send.at[ll], adj_recv.at[line], along(ll),
            )
    for ll in others:
        arrived(from_adjoint.at[group(ll)], adj_recv.at[ll])
        solved += from_adjoint[group(ll)].reshape(chunks * width, lanes).astype(F32)

    def share(pp, ll):
        block = field_ref.at[pp, group(ll, base)]
        push(block, block, sib_send.at[pp, ll], sib_recv.at[pp, ll], sibling)

    def share_across(ll):
        block = field_ref.at[part, group(ll, base)]
        for pp in parts:
            push(block, block, sol_x_send.at[pp, ll], sol_x_recv.at[part, ll], across(pp))

    field_ref[part, group(line, base)] = solved.astype(BF16).reshape(chunks, width, lanes)
    own = field_ref.at[part, group(line, base)]
    for ll in others:
        push(own, own, sol_send.at[ll], sol_recv.at[line], along(ll))
    share_across(line)
    share(part, line)
    for ll in others:
        arrived(field_ref.at[part, group(ll, base)], sol_recv.at[ll])
        share_across(ll)
        share(part, ll)
    for ll in others:
        push(
            gathered_fwd.at[mine], gathered_fwd.at[mine],
            fwd_send.at[ll], fwd_recv.at[line], along(ll),
        )
    for ll in [line] + others:
        for pp in parts:
            arrived(field_ref.at[pp, group(ll, base)], sol_x_recv.at[pp, ll])
            share(pp, ll)
    for c in range(chunks):
        solution_ref[0, :, c * lanes : (c + 1) * lanes] = field_ref[c, base + me].astype(F32)

    for ll in others:
        arrived(gathered_fwd.at[group(ll)], fwd_recv.at[ll])

    def forward_of(sep):
        slot = jnp.int32(0)
        for p in range(fronts):
            slot = jnp.where(order_ref[0, p] == sep, p, slot)
        return gathered_fwd[slot]

    from_peer[part] = forward_of(me)
    for pp in parts:
        to_peer[pp] = forward_of(line * chunks + pp)
        push(to_peer.at[pp], from_peer.at[part], peer_send.at[pp], peer_recv.at[part], across(pp))
    for pp in parts + [part]:
        for ll in [line] + others:
            arrived(field_ref.at[pp, group(ll, far_base)], sib_recv.at[pp, ll])
    for pp in parts:
        arrived(from_peer.at[pp], peer_recv.at[pp])
    for c in range(chunks):
        forward_ref[0, :, c * lanes : (c + 1) * lanes] = from_peer[c]
    for copy in sent:
        copy.wait_send()


def on_device(
    leaf_inverse, leaf_rhs, off_blocks, block_rows, fill_count, sep_rhs, panel_order, sep_inverse
):
    leaves, width = leaf_inverse.shape[:2]
    probes = leaf_rhs.shape[2]
    slots = off_blocks.shape[1]
    fronts = lax.axis_size("front")
    steps = leaves // LEAF_STEP
    block = (width, probes)
    lanes = 128
    chunks = probes // lanes
    piece = (width, lanes)
    lines = fronts // chunks
    rows = block_rows.T
    panel = sep_inverse.reshape(width, fronts * width)

    smem = pl.BlockSpec(memory_space=pltpu.SMEM)
    vmem = pl.BlockSpec(memory_space=pltpu.VMEM)
    inverse_spec = pl.BlockSpec((LEAF_STEP, width, width), lambda i: (i, 0, 0))
    vector_spec = pl.BlockSpec((LEAF_STEP,) + block, lambda i: (i, 0, 0))
    off_spec = pl.BlockSpec((LEAF_STEP, slots, width, width), lambda i: (i, 0, 0, 0))
    turned_spec = pl.BlockSpec((LEAF_STEP, width, (slots + 1) * width), lambda i: (i, 0, 0))
    field_spec = pl.BlockSpec((chunks, 2 * fronts) + piece, lambda i: (0, 0, 0, 0))
    one_spec = pl.BlockSpec((1,) + block, lambda i: (0, 0, 0))
    flops = 2 * leaves * (slots + 1) * width * width * probes
    moved = 2 * leaves * width * (width * (slots + 1) + 2 * probes)
    cost = pl.CostEstimate(flops=flops, bytes_accessed=moved, transcendentals=0)

    forward, turned, partial = pl.pallas_call(
        leaf_forward,
        grid=(steps,),
        out_shape=(
            jax.ShapeDtypeStruct((leaves,) + block, BF16),
            jax.ShapeDtypeStruct((leaves, width, (slots + 1) * width), BF16),
            jax.ShapeDtypeStruct((chunks, 2 * fronts) + piece, BF16),
        ),
        in_specs=[smem, smem, inverse_spec, vector_spec, off_spec],
        out_specs=(vector_spec, turned_spec, field_spec),
        scratch_shapes=[pltpu.VMEM((2 * fronts + 1, width // 2, lanes), F32)] * (2 * chunks),
        compiler_params=pltpu.CompilerParams(vmem_limit_bytes=VMEM_BYTES),
        cost_estimate=cost,
        name="leaf_forward",
    )(rows, fill_count, leaf_inverse, leaf_rhs, off_blocks)

    dma = pltpu.SemaphoreType.DMA
    by_line, by_both = dma((lines,)), dma((chunks, lines))
    whole = pltpu.VMEM((chunks, fronts) + piece, BF16)
    part = pltpu.VMEM((fronts,) + piece, BF16)
    small = pltpu.VMEM((chunks,) + piece, BF16)

    field, sep_forward, sep_solution = pl.pallas_call(
        separators,
        out_shape=(
            jax.ShapeDtypeStruct((chunks, 2 * fronts) + piece, BF16),
            jax.ShapeDtypeStruct((1,) + block, BF16),
            jax.ShapeDtypeStruct((1,) + block, F32),
        ),
        in_specs=[smem, vmem, vmem, vmem],
        out_specs=(vmem, vmem, vmem),
        scratch_shapes=[
            whole, whole, whole, part, part, part, part, part, part, small, small,
            pltpu.VMEM((fronts * width, chunks * width), BF16),
            pltpu.VMEM((chunks, width, fronts * width), BF16),
            by_both, by_both, by_both, by_both, by_line, by_line, by_line, by_line,
            by_line, by_line, by_line, by_line, by_line, by_line, by_both, by_both,
            by_both, by_both, dma((chunks,)), dma((chunks,)), dma((chunks,)), dma((chunks,)),
        ],
        compiler_params=pltpu.CompilerParams(
            collective_id=0, has_side_effects=True, vmem_limit_bytes=VMEM_BYTES
        ),
        cost_estimate=pl.CostEstimate(
            flops=4 * fronts * width * width * probes,
            bytes_accessed=8 * fronts * width * probes,
            transcendentals=0,
        ),
        name="separators",
    )(panel_order, partial, sep_rhs, panel)

    return pl.pallas_call(
        leaf_backward,
        grid=(steps,),
        out_shape=(
            jax.ShapeDtypeStruct((leaves,) + block, BF16),
            jax.ShapeDtypeStruct((1,) + block, BF16),
            jax.ShapeDtypeStruct((1,) + block, F32),
        ),
        in_specs=[
            smem, smem, field_spec, turned_spec, vector_spec, one_spec, one_spec,
        ],
        out_specs=(vector_spec, one_spec, one_spec),
        compiler_params=pltpu.CompilerParams(vmem_limit_bytes=VMEM_BYTES),
        cost_estimate=cost,
        name="leaf_backward",
    )(rows, fill_count, field, turned, forward, sep_forward, sep_solution)


def solution(mesh):
    placed = (
        P(("leaf", "front"), None, None),
        P(("leaf", "front"), None, None),
        P(("leaf", "front"), None, None, None),
        P(("leaf", "front"), None),
        P(("leaf", "front")),
        P(("leaf", "front"), None, None),
        P("leaf", None),
        P(("leaf", "front"), None, None),
    )
    return jax.shard_map(
        on_device,
        mesh=mesh,
        in_specs=placed,
        out_specs=(
            P(("leaf", "front"), None, None),
            P(("leaf", "front"), None, None),
            P(("leaf", "front"), None, None),
        ),
        check_vma=False,
    )
```

```python
import jax
import jax.numpy as jnp
from jax import lax
from jax.experimental import pallas as pl
from jax.experimental.pallas import tpu as pltpu
from jax.sharding import PartitionSpec as P

MESH = pl.DeviceIdType.MESH
F32 = jnp.float32
BF16 = jnp.bfloat16
LEAF_STEP = 8
VMEM_BYTES = 56 * 1024 * 1024


def leaf_forward(
    rows_ref, fill_ref, inverse_ref, rhs_ref, off_ref, forward_ref, turned_ref, partial_ref, *accs
):
    step = pl.program_id(0)
    chunks, seps, _, lanes = partial_ref.shape
    slots, width = off_ref.shape[1], off_ref.shape[2]
    bands = len(accs) // chunks
    band = width // bands

    @pl.when(step == 0)
    def _():
        for acc in accs:
            acc[...] = jnp.zeros_like(acc)

    for i in range(LEAF_STEP):
        forward_ref[i] = jnp.dot(
            inverse_ref[i], rhs_ref[i], preferred_element_type=F32
        ).astype(BF16)
    for i in range(LEAF_STEP):
        leaf = step * LEAF_STEP + i
        stacked = off_ref[i].reshape(slots * width, width)
        product = jnp.dot(stacked, forward_ref[i], preferred_element_type=F32)
        turned_ref[i, :, : slots * width] = stacked.T
        turned_ref[i, :, slots * width :] = inverse_ref[i].T
        for p in range(slots):
            target = jnp.where(p < fill_ref[leaf], rows_ref[p, leaf], seps)
            for k, acc in enumerate(accs):
                c, top = k % chunks, p * width + k // chunks * band
                acc[target] += product[top : top + band, c * lanes : (c + 1) * lanes]

    @pl.when(step == pl.num_programs(0) - 1)
    def _():
        for k, acc in enumerate(accs):
            top = k // chunks * band
            partial_ref[k % chunks, :, top : top + band, :] = acc[:seps].astype(BF16)


def leaf_backward(
    rows_ref, fill_ref, field_ref, turned_ref, forward_ref, sep_fwd_ref, sep_sol_ref,
    out_ref, sep_fwd_out, sep_sol_out, backward,
):
    step = pl.program_id(0)
    slots, width = rows_ref.shape[0], turned_ref.shape[1]

    @pl.when(step == 0)
    def _():
        sep_fwd_out[...] = sep_fwd_ref[...]
        sep_sol_out[...] = sep_sol_ref[...]

    for i in range(LEAF_STEP):
        leaf = step * LEAF_STEP + i
        picked = []
        for p in range(slots):
            row = rows_ref[p, leaf]
            block = jnp.concatenate([field_ref[c, row] for c in range(field_ref.shape[0])], axis=1)
            picked.append(jnp.where(p < fill_ref[leaf], block, jnp.zeros_like(block)))
        pulled = jnp.dot(
            turned_ref[i, :, : slots * width],
            jnp.concatenate(picked, axis=0),
            preferred_element_type=F32,
        )
        backward[i] = (forward_ref[i].astype(F32) - pulled).astype(BF16)
    for i in range(LEAF_STEP):
        out_ref[i] = jnp.dot(
            turned_ref[i, :, slots * width :], backward[i], preferred_element_type=F32
        ).astype(BF16)


def separators(
    order_ref, partial_ref, rhs_ref, panel_ref,
    field_ref, forward_ref, solution_ref,
    from_core, to_x, from_x, to_z, from_z, gathered_in, to_adjoint, from_adjoint, gathered_fwd,
    to_peer, from_peer, panel_t, peer_panel,
    core_send, core_recv, x_send, x_recv, z_send, z_recv, in_send, in_recv, adj_send, adj_recv,
    fwd_send, fwd_recv, sol_send, sol_recv, sol_x_send, sol_x_recv, sib_send, sib_recv,
    peer_send, peer_recv, panel_send, panel_recv,
):
    chunks, seps, width, lanes = partial_ref.shape
    fronts = seps // 2
    lines = fronts // chunks
    leaf, me = lax.axis_index("leaf"), lax.axis_index("front")
    half = lax.rem(leaf, 2)
    line, part = me // chunks, lax.rem(me, chunks)
    base, far_base = half * fronts, (1 - half) * fronts
    sibling = (leaf + 1 - 2 * half, me)
    others = [lax.rem(line + k, lines) for k in range(1, lines)]
    parts = [lax.rem(part + k, chunks) for k in range(1, chunks)]
    order = others + [line]

    def along(ll):
        return (leaf, ll * chunks + part)

    def across(pp):
        return (leaf, line * chunks + pp)

    def group(ll, start=0):
        return pl.ds(start + ll * chunks, chunks)

    barrier = pltpu.get_barrier_semaphore()
    peers = [along(ll) for ll in others] + [across(pp) for pp in parts] + [sibling]
    for peer in peers:
        pl.semaphore_signal(barrier, inc=1, device_id=peer, device_id_type=MESH)
    pl.semaphore_wait(barrier, len(peers))

    sent = []

    def remote(src, dst, send, recv, device):
        return pltpu.make_async_remote_copy(
            src_ref=src, dst_ref=dst, send_sem=send, recv_sem=recv,
            device_id=device, device_id_type=MESH,
        )

    def push(src, dst, send, recv, device):
        copy = remote(src, dst, send, recv, device)
        copy.start()
        sent.append(copy)

    def arrived(dst, recv):
        remote(dst, dst, recv, recv, sibling).wait_recv()

    rhs = [rhs_ref[0, :, c * lanes : (c + 1) * lanes].astype(F32) for c in range(chunks)]

    def rhs_of(pp):
        value = rhs[0]
        for c in range(1, chunks):
            value = jnp.where(pp == c, rhs[c], value)
        return value

    for pp in parts + [part]:
        for ll in order:
            push(
                partial_ref.at[pp, group(ll, far_base)], from_core.at[pp, group(ll)],
                core_send.at[pp, ll], core_recv.at[pp, ll], sibling,
            )

    def pair_sum(pp, f):
        return partial_ref[pp, base + f].astype(F32) + from_core[pp, f].astype(F32)

    for pp in parts:
        for ll in order:
            arrived(from_core.at[pp, group(ll)], core_recv.at[pp, ll])
            for k in range(chunks):
                f = ll * chunks + k
                value = pair_sum(pp, f)
                if ll is line:
                    value = jnp.where(part == k, value - rhs_of(pp), value)
                to_x[pp, f] = value.astype(BF16)
            push(
                to_x.at[pp, group(ll)], from_x.at[part, group(ll)],
                x_send.at[pp, ll], x_recv.at[part, ll], across(pp),
            )
    for pp in parts:
        push(panel_ref, peer_panel.at[part], panel_send.at[pp], panel_recv.at[part], across(pp))
    totals = []
    for ll in order:
        arrived(from_core.at[part, group(ll)], core_recv.at[part, ll])
        for pp in parts:
            arrived(from_x.at[pp, group(ll)], x_recv.at[pp, ll])
        for k in range(chunks):
            f = ll * chunks + k
            value = pair_sum(part, f)
            for pp in parts:
                value += from_x[pp, f].astype(F32)
            if ll is line:
                totals.append(jnp.where(part == k, value - rhs_of(part), value))
            else:
                to_z[f] = value.astype(BF16)
        if ll is not line:
            push(to_z.at[group(ll)], from_z.at[group(line)], z_send.at[ll], z_recv.at[line], along(ll))
    for ll in others:
        arrived(from_z.at[group(ll)], z_recv.at[ll])
        for k in range(chunks):
            totals[k] += from_z[ll * chunks + k].astype(F32)

    for k in range(chunks):
        gathered_in[line * chunks + k] = (-totals[k]).astype(BF16)
    mine = group(line)
    for ll in others:
        push(gathered_in.at[mine], gathered_in.at[mine], in_send.at[ll], in_recv.at[line], along(ll))

    for pp in parts:
        arrived(peer_panel.at[pp], panel_recv.at[pp])
    panels = [panel_ref] + [peer_panel.at[pp] for pp in parts]
    for f in range(fronts):
        for k, panel in enumerate(panels):
            panel_t[f * width : (f + 1) * width, k * width : (k + 1) * width] = panel[
                :, f * width : (f + 1) * width
            ].T

    forward = [jnp.zeros((width, lanes), F32)] * chunks
    for ll in [line] + others:
        if ll is not line:
            arrived(gathered_in.at[group(ll)], in_recv.at[ll])
        vectors = gathered_in[group(ll)].reshape(chunks * width, lanes)
        columns = pl.ds(pl.multiple_of(ll * chunks * width, chunks * width), chunks * width)
        for k, panel in enumerate(panels):
            forward[k] += jnp.dot(panel[:, columns], vectors, preferred_element_type=F32)
    forward = [value.astype(BF16) for value in forward]
    stacked = jnp.concatenate(forward, axis=0)
    for k in range(chunks):
        gathered_fwd[line * chunks + lax.rem(part + k, chunks)] = forward[k]

    solved = None
    for ll in order:
        rows = pl.ds(pl.multiple_of(ll * chunks * width, chunks * width), chunks * width)
        term = jnp.dot(panel_t[rows, :], stacked, preferred_element_type=F32)
        if ll is line:
            solved = term
        else:
            to_adjoint[group(ll)] = term.astype(BF16).reshape(chunks, width, lanes)
            push(
                to_adjoint.at[group(ll)], from_adjoint.at[mine],
                adj_send.at[ll], adj_recv.at[line], along(ll),
            )
    for ll in others:
        arrived(from_adjoint.at[group(ll)], adj_recv.at[ll])
        solved += from_adjoint[group(ll)].reshape(chunks * width, lanes).astype(F32)

    def share(pp, ll):
        block = field_ref.at[pp, group(ll, base)]
        push(block, block, sib_send.at[pp, ll], sib_recv.at[pp, ll], sibling)

    def share_across(ll):
        block = field_ref.at[part, group(ll, base)]
        for pp in parts:
            push(block, block, sol_x_send.at[pp, ll], sol_x_recv.at[part, ll], across(pp))

    field_ref[part, group(line, base)] = solved.astype(BF16).reshape(chunks, width, lanes)
    own = field_ref.at[part, group(line, base)]
    for ll in others:
        push(own, own, sol_send.at[ll], sol_recv.at[line], along(ll))
    share_across(line)
    share(part, line)
    for ll in others:
        push(
            gathered_fwd.at[mine], gathered_fwd.at[mine],
            fwd_send.at[ll], fwd_recv.at[line], along(ll),
        )
    for ll in others:
        arrived(field_ref.at[part, group(ll, base)], sol_recv.at[ll])
        share_across(ll)
        share(part, ll)
    for ll in [line] + others:
        for pp in parts:
            arrived(field_ref.at[pp, group(ll, base)], sol_x_recv.at[pp, ll])
            share(pp, ll)
    for c in range(chunks):
        solution_ref[0, :, c * lanes : (c + 1) * lanes] = field_ref[c, base + me].astype(F32)

    for ll in others:
        arrived(gathered_fwd.at[group(ll)], fwd_recv.at[ll])

    def forward_of(sep):
        slot = jnp.int32(0)
        for p in range(fronts):
            slot = jnp.where(order_ref[0, p] == sep, p, slot)
        return gathered_fwd[slot]

    from_peer[part] = forward_of(me)
    for pp in parts:
        to_peer[pp] = forward_of(line * chunks + pp)
        push(to_peer.at[pp], from_peer.at[part], peer_send.at[pp], peer_recv.at[part], across(pp))
    for pp in parts + [part]:
        for ll in [line] + others:
            arrived(field_ref.at[pp, group(ll, far_base)], sib_recv.at[pp, ll])
    for pp in parts:
        arrived(from_peer.at[pp], peer_recv.at[pp])
    for c in range(chunks):
        forward_ref[0, :, c * lanes : (c + 1) * lanes] = from_peer[c]
    for copy in sent:
        copy.wait_send()


def on_device(
    leaf_inverse, leaf_rhs, off_blocks, block_rows, fill_count, sep_rhs, panel_order, sep_inverse
):
    leaves, width = leaf_inverse.shape[:2]
    probes = leaf_rhs.shape[2]
    slots = off_blocks.shape[1]
    fronts = lax.axis_size("front")
    steps = leaves // LEAF_STEP
    block = (width, probes)
    lanes = 128
    chunks = probes // lanes
    piece = (width, lanes)
    lines = fronts // chunks
    rows = block_rows.T
    panel = sep_inverse.reshape(width, fronts * width)

    smem = pl.BlockSpec(memory_space=pltpu.SMEM)
    vmem = pl.BlockSpec(memory_space=pltpu.VMEM)
    inverse_spec = pl.BlockSpec((LEAF_STEP, width, width), lambda i: (i, 0, 0))
    vector_spec = pl.BlockSpec((LEAF_STEP,) + block, lambda i: (i, 0, 0))
    off_spec = pl.BlockSpec((LEAF_STEP, slots, width, width), lambda i: (i, 0, 0, 0))
    turned_spec = pl.BlockSpec((LEAF_STEP, width, (slots + 1) * width), lambda i: (i, 0, 0))
    field_spec = pl.BlockSpec((chunks, 2 * fronts) + piece, lambda i: (0, 0, 0, 0))
    one_spec = pl.BlockSpec((1,) + block, lambda i: (0, 0, 0))
    flops = 2 * leaves * (slots + 1) * width * width * probes
    moved = 2 * leaves * width * (width * (slots + 1) + 2 * probes)
    cost = pl.CostEstimate(flops=flops, bytes_accessed=moved, transcendentals=0)

    forward, turned, partial = pl.pallas_call(
        leaf_forward,
        grid=(steps,),
        out_shape=(
            jax.ShapeDtypeStruct((leaves,) + block, BF16),
            jax.ShapeDtypeStruct((leaves, width, (slots + 1) * width), BF16),
            jax.ShapeDtypeStruct((chunks, 2 * fronts) + piece, BF16),
        ),
        in_specs=[smem, smem, inverse_spec, vector_spec, off_spec],
        out_specs=(vector_spec, turned_spec, field_spec),
        scratch_shapes=[pltpu.VMEM((2 * fronts + 1, width // 2, lanes), F32)] * (2 * chunks),
        compiler_params=pltpu.CompilerParams(vmem_limit_bytes=VMEM_BYTES),
        cost_estimate=cost,
        name="leaf_forward",
    )(rows, fill_count, leaf_inverse, leaf_rhs, off_blocks)

    dma = pltpu.SemaphoreType.DMA
    by_line, by_both = dma((lines,)), dma((chunks, lines))
    whole = pltpu.VMEM((chunks, fronts) + piece, BF16)
    part = pltpu.VMEM((fronts,) + piece, BF16)
    small = pltpu.VMEM((chunks,) + piece, BF16)

    field, sep_forward, sep_solution = pl.pallas_call(
        separators,
        out_shape=(
            jax.ShapeDtypeStruct((chunks, 2 * fronts) + piece, BF16),
            jax.ShapeDtypeStruct((1,) + block, BF16),
            jax.ShapeDtypeStruct((1,) + block, F32),
        ),
        in_specs=[smem, vmem, vmem, vmem],
        out_specs=(vmem, vmem, vmem),
        scratch_shapes=[
            whole, whole, whole, part, part, part, part, part, part, small, small,
            pltpu.VMEM((fronts * width, chunks * width), BF16),
            pltpu.VMEM((chunks, width, fronts * width), BF16),
            by_both, by_both, by_both, by_both, by_line, by_line, by_line, by_line,
            by_line, by_line, by_line, by_line, by_line, by_line, by_both, by_both,
            by_both, by_both, dma((chunks,)), dma((chunks,)), dma((chunks,)), dma((chunks,)),
        ],
        compiler_params=pltpu.CompilerParams(
            collective_id=0, has_side_effects=True, vmem_limit_bytes=VMEM_BYTES
        ),
        cost_estimate=pl.CostEstimate(
            flops=4 * fronts * width * width * probes,
            bytes_accessed=8 * fronts * width * probes,
            transcendentals=0,
        ),
        name="separators",
    )(panel_order, partial, sep_rhs, panel)

    return pl.pallas_call(
        leaf_backward,
        grid=(steps,),
        out_shape=(
            jax.ShapeDtypeStruct((leaves,) + block, BF16),
            jax.ShapeDtypeStruct((1,) + block, BF16),
            jax.ShapeDtypeStruct((1,) + block, F32),
        ),
        in_specs=[
            smem, smem, field_spec, turned_spec, vector_spec, one_spec, one_spec,
        ],
        out_specs=(vector_spec, one_spec, one_spec),
        scratch_shapes=[pltpu.VMEM((LEAF_STEP,) + block, BF16)],
        compiler_params=pltpu.CompilerParams(vmem_limit_bytes=VMEM_BYTES),
        cost_estimate=cost,
        name="leaf_backward",
    )(rows, fill_count, field, turned, forward, sep_forward, sep_solution)


def solution(mesh):
    placed = (
        P(("leaf", "front"), None, None),
        P(("leaf", "front"), None, None),
        P(("leaf", "front"), None, None, None),
        P(("leaf", "front"), None),
        P(("leaf", "front")),
        P(("leaf", "front"), None, None),
        P("leaf", None),
        P(("leaf", "front"), None, None),
    )
    return jax.shard_map(
        on_device,
        mesh=mesh,
        in_specs=placed,
        out_specs=(
            P(("leaf", "front"), None, None),
            P(("leaf", "front"), None, None),
            P(("leaf", "front"), None, None),
        ),
        check_vma=False,
    )
```

```python
import jax
import jax.numpy as jnp
from jax import lax
from jax.experimental import pallas as pl
from jax.experimental.pallas import tpu as pltpu
from jax.sharding import PartitionSpec as P

MESH = pl.DeviceIdType.MESH
F32 = jnp.float32
BF16 = jnp.bfloat16
LEAF_STEP = 8
VMEM_BYTES = 56 * 1024 * 1024


def leaf_forward(
    rows_ref, fill_ref, inverse_ref, rhs_ref, off_ref, forward_ref, turned_ref, partial_ref, *accs
):
    step = pl.program_id(0)
    chunks, seps, _, lanes = partial_ref.shape
    slots, width = off_ref.shape[1], off_ref.shape[2]
    bands = len(accs) // chunks
    band = width // bands

    @pl.when(step == 0)
    def _():
        for acc in accs:
            acc[...] = jnp.zeros_like(acc)

    for i in range(LEAF_STEP):
        forward_ref[i] = jnp.dot(
            inverse_ref[i], rhs_ref[i], preferred_element_type=F32
        ).astype(BF16)
    for i in range(LEAF_STEP):
        leaf = step * LEAF_STEP + i
        stacked = off_ref[i].reshape(slots * width, width)
        product = jnp.dot(stacked, forward_ref[i], preferred_element_type=F32)
        turned_ref[i, :, : slots * width] = stacked.T
        turned_ref[i, :, slots * width :] = inverse_ref[i].T
        for p in range(slots):
            target = jnp.where(p < fill_ref[leaf], rows_ref[p, leaf], seps)
            for k, acc in enumerate(accs):
                c, top = k % chunks, p * width + k // chunks * band
                acc[target] += product[top : top + band, c * lanes : (c + 1) * lanes]

    @pl.when(step == pl.num_programs(0) - 1)
    def _():
        for k, acc in enumerate(accs):
            top = k // chunks * band
            partial_ref[k % chunks, :, top : top + band, :] = acc[:seps].astype(BF16)


def separators(
    rows_ref, fill_ref, order_ref, partial_ref, rhs_ref, panel_ref, turned_hbm, leaf_forward_hbm,
    leaf_hbm, forward_ref, solution_ref,
    turned_ref, leaf_forward_ref, backward, leaf_out, load_sems, store_sems, field_ref,
    from_core, to_x, from_x, to_z, from_z, gathered_in, to_adjoint, from_adjoint, gathered_fwd,
    to_peer, from_peer, panel_t, peer_panel,
    core_send, core_recv, x_send, x_recv, z_send, z_recv, in_send, in_recv, adj_send, adj_recv,
    fwd_send, fwd_recv, sol_send, sol_recv, sol_x_send, sol_x_recv, sib_send, sib_recv,
    peer_send, peer_recv, panel_send, panel_recv,
):
    loads = [
        pltpu.make_async_copy(turned_hbm, turned_ref, load_sems.at[0]),
        pltpu.make_async_copy(leaf_forward_hbm, leaf_forward_ref, load_sems.at[1]),
    ]
    for load in loads:
        load.start()
    chunks, seps, width, lanes = partial_ref.shape
    slots = rows_ref.shape[0]
    fronts = seps // 2
    lines = fronts // chunks
    leaf, me = lax.axis_index("leaf"), lax.axis_index("front")
    half = lax.rem(leaf, 2)
    line, part = me // chunks, lax.rem(me, chunks)
    base, far_base = half * fronts, (1 - half) * fronts
    sibling = (leaf + 1 - 2 * half, me)
    others = [lax.rem(line + k, lines) for k in range(1, lines)]
    parts = [lax.rem(part + k, chunks) for k in range(1, chunks)]
    order = others + [line]

    def along(ll):
        return (leaf, ll * chunks + part)

    def across(pp):
        return (leaf, line * chunks + pp)

    def group(ll, start=0):
        return pl.ds(start + ll * chunks, chunks)

    barrier = pltpu.get_barrier_semaphore()
    peers = [along(ll) for ll in others] + [across(pp) for pp in parts] + [sibling]
    for peer in peers:
        pl.semaphore_signal(barrier, inc=1, device_id=peer, device_id_type=MESH)
    pl.semaphore_wait(barrier, len(peers))

    sent = []

    def remote(src, dst, send, recv, device):
        return pltpu.make_async_remote_copy(
            src_ref=src, dst_ref=dst, send_sem=send, recv_sem=recv,
            device_id=device, device_id_type=MESH,
        )

    def push(src, dst, send, recv, device):
        copy = remote(src, dst, send, recv, device)
        copy.start()
        sent.append(copy)

    def arrived(dst, recv):
        remote(dst, dst, recv, recv, sibling).wait_recv()

    rhs = [rhs_ref[0, :, c * lanes : (c + 1) * lanes].astype(F32) for c in range(chunks)]

    def rhs_of(pp):
        value = rhs[0]
        for c in range(1, chunks):
            value = jnp.where(pp == c, rhs[c], value)
        return value

    for pp in parts + [part]:
        for ll in order:
            push(
                partial_ref.at[pp, group(ll, far_base)], from_core.at[pp, group(ll)],
                core_send.at[pp, ll], core_recv.at[pp, ll], sibling,
            )

    def pair_sum(pp, f):
        return partial_ref[pp, base + f].astype(F32) + from_core[pp, f].astype(F32)

    for pp in parts:
        for ll in order:
            arrived(from_core.at[pp, group(ll)], core_recv.at[pp, ll])
            for k in range(chunks):
                f = ll * chunks + k
                value = pair_sum(pp, f)
                if ll is line:
                    value = jnp.where(part == k, value - rhs_of(pp), value)
                to_x[pp, f] = value.astype(BF16)
            push(
                to_x.at[pp, group(ll)], from_x.at[part, group(ll)],
                x_send.at[pp, ll], x_recv.at[part, ll], across(pp),
            )
    for pp in parts:
        push(panel_ref, peer_panel.at[part], panel_send.at[pp], panel_recv.at[part], across(pp))
    totals = []
    for ll in order:
        arrived(from_core.at[part, group(ll)], core_recv.at[part, ll])
        for pp in parts:
            arrived(from_x.at[pp, group(ll)], x_recv.at[pp, ll])
        for k in range(chunks):
            f = ll * chunks + k
            value = pair_sum(part, f)
            for pp in parts:
                value += from_x[pp, f].astype(F32)
            if ll is line:
                totals.append(jnp.where(part == k, value - rhs_of(part), value))
            else:
                to_z[f] = value.astype(BF16)
        if ll is not line:
            push(to_z.at[group(ll)], from_z.at[group(line)], z_send.at[ll], z_recv.at[line], along(ll))
    for ll in others:
        arrived(from_z.at[group(ll)], z_recv.at[ll])
        for k in range(chunks):
            totals[k] += from_z[ll * chunks + k].astype(F32)

    for k in range(chunks):
        gathered_in[line * chunks + k] = (-totals[k]).astype(BF16)
    mine = group(line)
    for ll in others:
        push(gathered_in.at[mine], gathered_in.at[mine], in_send.at[ll], in_recv.at[line], along(ll))

    for pp in parts:
        arrived(peer_panel.at[pp], panel_recv.at[pp])
    panels = [panel_ref] + [peer_panel.at[pp] for pp in parts]
    for f in range(fronts):
        for k, panel in enumerate(panels):
            panel_t[f * width : (f + 1) * width, k * width : (k + 1) * width] = panel[
                :, f * width : (f + 1) * width
            ].T

    forward = [jnp.zeros((width, lanes), F32)] * chunks
    for ll in [line] + others:
        if ll is not line:
            arrived(gathered_in.at[group(ll)], in_recv.at[ll])
        vectors = gathered_in[group(ll)].reshape(chunks * width, lanes)
        columns = pl.ds(pl.multiple_of(ll * chunks * width, chunks * width), chunks * width)
        for k, panel in enumerate(panels):
            forward[k] += jnp.dot(panel[:, columns], vectors, preferred_element_type=F32)
    forward = [value.astype(BF16) for value in forward]
    stacked = jnp.concatenate(forward, axis=0)
    for k in range(chunks):
        gathered_fwd[line * chunks + lax.rem(part + k, chunks)] = forward[k]

    solved = None
    for ll in order:
        rows = pl.ds(pl.multiple_of(ll * chunks * width, chunks * width), chunks * width)
        term = jnp.dot(panel_t[rows, :], stacked, preferred_element_type=F32)
        if ll is line:
            solved = term
        else:
            to_adjoint[group(ll)] = term.astype(BF16).reshape(chunks, width, lanes)
            push(
                to_adjoint.at[group(ll)], from_adjoint.at[mine],
                adj_send.at[ll], adj_recv.at[line], along(ll),
            )
    for ll in others:
        arrived(from_adjoint.at[group(ll)], adj_recv.at[ll])
        solved += from_adjoint[group(ll)].reshape(chunks * width, lanes).astype(F32)

    def share(pp, ll):
        block = field_ref.at[pp, group(ll, base)]
        push(block, block, sib_send.at[pp, ll], sib_recv.at[pp, ll], sibling)

    def share_across(ll):
        block = field_ref.at[part, group(ll, base)]
        for pp in parts:
            push(block, block, sol_x_send.at[pp, ll], sol_x_recv.at[part, ll], across(pp))

    field_ref[part, group(line, base)] = solved.astype(BF16).reshape(chunks, width, lanes)
    own = field_ref.at[part, group(line, base)]
    for ll in others:
        push(own, own, sol_send.at[ll], sol_recv.at[line], along(ll))
    share_across(line)
    share(part, line)
    for ll in others:
        arrived(field_ref.at[part, group(ll, base)], sol_recv.at[ll])
        share_across(ll)
        share(part, ll)
    for ll in others:
        push(
            gathered_fwd.at[mine], gathered_fwd.at[mine],
            fwd_send.at[ll], fwd_recv.at[line], along(ll),
        )
    for ll in [line] + others:
        for pp in parts:
            arrived(field_ref.at[pp, group(ll, base)], sol_x_recv.at[pp, ll])
            share(pp, ll)
    for c in range(chunks):
        solution_ref[0, :, c * lanes : (c + 1) * lanes] = field_ref[c, base + me].astype(F32)

    for pp in parts + [part]:
        for ll in [line] + others:
            arrived(field_ref.at[pp, group(ll, far_base)], sib_recv.at[pp, ll])
    for load in loads:
        load.wait()

    def leaf_store(step):
        some = pl.ds(step * LEAF_STEP, LEAF_STEP)
        return pltpu.make_async_copy(leaf_out.at[some], leaf_hbm.at[some], store_sems.at[step])

    def leaf_step(step, carry):
        for i in range(LEAF_STEP):
            leaf = step * LEAF_STEP + i
            picked = []
            for p in range(slots):
                row = rows_ref[p, leaf]
                block = jnp.concatenate([field_ref[c, row] for c in range(chunks)], axis=1)
                picked.append(jnp.where(p < fill_ref[leaf], block, jnp.zeros_like(block)))
            pulled = jnp.dot(
                turned_ref[leaf, :, : slots * width],
                jnp.concatenate(picked, axis=0),
                preferred_element_type=F32,
            )
            backward[i] = (leaf_forward_ref[leaf].astype(F32) - pulled).astype(BF16)
        for i in range(LEAF_STEP):
            leaf = step * LEAF_STEP + i
            leaf_out[leaf] = jnp.dot(
                turned_ref[leaf, :, slots * width :], backward[i], preferred_element_type=F32
            ).astype(BF16)
        leaf_store(step).start()
        return carry

    steps = leaf_out.shape[0] // LEAF_STEP
    lax.fori_loop(0, steps // 2, leaf_step, 0)

    for ll in others:
        arrived(gathered_fwd.at[group(ll)], fwd_recv.at[ll])

    def forward_of(sep):
        slot = jnp.int32(0)
        for p in range(fronts):
            slot = jnp.where(order_ref[0, p] == sep, p, slot)
        return gathered_fwd[slot]

    from_peer[part] = forward_of(me)
    for pp in parts:
        to_peer[pp] = forward_of(line * chunks + pp)
        push(to_peer.at[pp], from_peer.at[part], peer_send.at[pp], peer_recv.at[part], across(pp))
    lax.fori_loop(steps // 2, steps, leaf_step, 0)
    for pp in parts:
        arrived(from_peer.at[pp], peer_recv.at[pp])
    for c in range(chunks):
        forward_ref[0, :, c * lanes : (c + 1) * lanes] = from_peer[c]
    for step in range(steps):
        leaf_store(step).wait()
    for copy in sent:
        copy.wait_send()


def on_device(
    leaf_inverse, leaf_rhs, off_blocks, block_rows, fill_count, sep_rhs, panel_order, sep_inverse
):
    leaves, width = leaf_inverse.shape[:2]
    probes = leaf_rhs.shape[2]
    slots = off_blocks.shape[1]
    fronts = lax.axis_size("front")
    steps = leaves // LEAF_STEP
    block = (width, probes)
    lanes = 128
    chunks = probes // lanes
    piece = (width, lanes)
    lines = fronts // chunks
    rows = block_rows.T
    panel = sep_inverse.reshape(width, fronts * width)

    smem = pl.BlockSpec(memory_space=pltpu.SMEM)
    vmem = pl.BlockSpec(memory_space=pltpu.VMEM)
    hbm = pl.BlockSpec(memory_space=pl.ANY)
    inverse_spec = pl.BlockSpec((LEAF_STEP, width, width), lambda i: (i, 0, 0))
    vector_spec = pl.BlockSpec((LEAF_STEP,) + block, lambda i: (i, 0, 0))
    off_spec = pl.BlockSpec((LEAF_STEP, slots, width, width), lambda i: (i, 0, 0, 0))
    turned_spec = pl.BlockSpec((LEAF_STEP, width, (slots + 1) * width), lambda i: (i, 0, 0))
    field_spec = pl.BlockSpec((chunks, 2 * fronts) + piece, lambda i: (0, 0, 0, 0))
    flops = 2 * leaves * (slots + 1) * width * width * probes
    moved = 2 * leaves * width * (width * (slots + 1) + 2 * probes)
    cost = pl.CostEstimate(flops=flops, bytes_accessed=moved, transcendentals=0)

    forward, turned, partial = pl.pallas_call(
        leaf_forward,
        grid=(steps,),
        out_shape=(
            jax.ShapeDtypeStruct((leaves,) + block, BF16),
            jax.ShapeDtypeStruct((leaves, width, (slots + 1) * width), BF16),
            jax.ShapeDtypeStruct((chunks, 2 * fronts) + piece, BF16),
        ),
        in_specs=[smem, smem, inverse_spec, vector_spec, off_spec],
        out_specs=(vector_spec, turned_spec, field_spec),
        scratch_shapes=[pltpu.VMEM((2 * fronts + 1, width // 2, lanes), F32)] * (2 * chunks),
        compiler_params=pltpu.CompilerParams(vmem_limit_bytes=VMEM_BYTES),
        cost_estimate=cost,
        name="leaf_forward",
    )(rows, fill_count, leaf_inverse, leaf_rhs, off_blocks)

    dma = pltpu.SemaphoreType.DMA
    by_line, by_both = dma((lines,)), dma((chunks, lines))
    whole = pltpu.VMEM((chunks, fronts) + piece, BF16)
    part = pltpu.VMEM((fronts,) + piece, BF16)
    small = pltpu.VMEM((chunks,) + piece, BF16)

    leaf_solution, sep_forward, sep_solution = pl.pallas_call(
        separators,
        out_shape=(
            jax.ShapeDtypeStruct((leaves,) + block, BF16),
            jax.ShapeDtypeStruct((1,) + block, BF16),
            jax.ShapeDtypeStruct((1,) + block, F32),
        ),
        in_specs=[smem, smem, smem, vmem, vmem, vmem, hbm, hbm],
        out_specs=(hbm, vmem, vmem),
        scratch_shapes=[
            pltpu.VMEM((leaves, width, (slots + 1) * width), BF16),
            pltpu.VMEM((leaves,) + block, BF16),
            pltpu.VMEM((LEAF_STEP,) + block, BF16),
            pltpu.VMEM((leaves,) + block, BF16),
            dma((2,)), dma((steps,)),
            pltpu.VMEM((chunks, 2 * fronts) + piece, BF16),
            whole, whole, whole, part, part, part, part, part, part, small, small,
            pltpu.VMEM((fronts * width, chunks * width), BF16),
            pltpu.VMEM((chunks, width, fronts * width), BF16),
            by_both, by_both, by_both, by_both, by_line, by_line, by_line, by_line,
            by_line, by_line, by_line, by_line, by_line, by_line, by_both, by_both,
            by_both, by_both, dma((chunks,)), dma((chunks,)), dma((chunks,)), dma((chunks,)),
        ],
        compiler_params=pltpu.CompilerParams(
            collective_id=0, has_side_effects=True, vmem_limit_bytes=VMEM_BYTES
        ),
        cost_estimate=cost,
        name="separators",
    )(rows, fill_count, panel_order, partial, sep_rhs, panel, turned, forward)
    return (leaf_solution, sep_forward, sep_solution)


def solution(mesh):
    placed = (
        P(("leaf", "front"), None, None),
        P(("leaf", "front"), None, None),
        P(("leaf", "front"), None, None, None),
        P(("leaf", "front"), None),
        P(("leaf", "front")),
        P(("leaf", "front"), None, None),
        P("leaf", None),
        P(("leaf", "front"), None, None),
    )
    return jax.shard_map(
        on_device,
        mesh=mesh,
        in_specs=placed,
        out_specs=(
            P(("leaf", "front"), None, None),
            P(("leaf", "front"), None, None),
            P(("leaf", "front"), None, None),
        ),
        check_vma=False,
    )
```

```python
import jax
import jax.numpy as jnp
from jax import lax
from jax.experimental import pallas as pl
from jax.experimental.pallas import tpu as pltpu
from jax.sharding import PartitionSpec as P

MESH = pl.DeviceIdType.MESH
F32 = jnp.float32
BF16 = jnp.bfloat16
LEAF_STEP = 8
FIRST_DIMS = (((0,), (0,)), ((), ()))
VMEM_BYTES = 56 * 1024 * 1024


def leaf_forward(
    rows_ref, fill_ref, inverse_ref, rhs_ref, off_ref, forward_ref, partial_ref, *accs
):
    step = pl.program_id(0)
    chunks, seps, _, lanes = partial_ref.shape
    slots, width = off_ref.shape[1], off_ref.shape[2]
    bands = len(accs) // chunks
    band = width // bands

    @pl.when(step == 0)
    def _():
        for acc in accs:
            acc[...] = jnp.zeros_like(acc)

    for i in range(LEAF_STEP):
        forward_ref[i] = jnp.dot(
            inverse_ref[i], rhs_ref[i], preferred_element_type=F32
        ).astype(BF16)
    for i in range(LEAF_STEP):
        leaf = step * LEAF_STEP + i
        stacked = off_ref[i].reshape(slots * width, width)
        product = jnp.dot(stacked, forward_ref[i], preferred_element_type=F32)
        for p in range(slots):
            target = jnp.where(p < fill_ref[leaf], rows_ref[p, leaf], seps)
            for k, acc in enumerate(accs):
                c, top = k % chunks, p * width + k // chunks * band
                acc[target] += product[top : top + band, c * lanes : (c + 1) * lanes]

    @pl.when(step == pl.num_programs(0) - 1)
    def _():
        for k, acc in enumerate(accs):
            top = k // chunks * band
            partial_ref[k % chunks, :, top : top + band, :] = acc[:seps].astype(BF16)


def leaf_finish(
    inverse_ref, backward_ref, sep_fwd_ref, sep_sol_ref, out_ref, sep_fwd_out, sep_sol_out
):
    @pl.when(pl.program_id(0) == 0)
    def _():
        sep_fwd_out[...] = sep_fwd_ref[...]
        sep_sol_out[...] = sep_sol_ref[...]

    for i in range(LEAF_STEP):
        out_ref[i] = lax.dot_general(
            inverse_ref[i], backward_ref[i], FIRST_DIMS, preferred_element_type=F32
        ).astype(BF16)


def separators(
    rows_ref, fill_ref, order_ref, partial_ref, rhs_ref, panel_ref, off_hbm, leaf_forward_hbm,
    leaf_hbm, forward_ref, solution_ref,
    off_ref, turned_ref, leaf_forward_ref, leaf_out, load_sems, store_sems, field_ref,
    from_core, to_x, from_x, to_z, from_z, gathered_in, to_adjoint, from_adjoint, gathered_fwd,
    to_peer, from_peer, panel_t, peer_panel,
    core_send, core_recv, x_send, x_recv, z_send, z_recv, in_send, in_recv, adj_send, adj_recv,
    fwd_send, fwd_recv, sol_send, sol_recv, sol_x_send, sol_x_recv, sib_send, sib_recv,
    peer_send, peer_recv, panel_send, panel_recv,
):
    loads = [
        pltpu.make_async_copy(off_hbm, off_ref, load_sems.at[0]),
        pltpu.make_async_copy(leaf_forward_hbm, leaf_forward_ref, load_sems.at[1]),
    ]
    for load in loads:
        load.start()
    chunks, seps, width, lanes = partial_ref.shape
    slots = rows_ref.shape[0]
    fronts = seps // 2
    lines = fronts // chunks
    leaf, me = lax.axis_index("leaf"), lax.axis_index("front")
    half = lax.rem(leaf, 2)
    line, part = me // chunks, lax.rem(me, chunks)
    base, far_base = half * fronts, (1 - half) * fronts
    sibling = (leaf + 1 - 2 * half, me)
    others = [lax.rem(line + k, lines) for k in range(1, lines)]
    parts = [lax.rem(part + k, chunks) for k in range(1, chunks)]
    order = others + [line]

    def along(ll):
        return (leaf, ll * chunks + part)

    def across(pp):
        return (leaf, line * chunks + pp)

    def group(ll, start=0):
        return pl.ds(start + ll * chunks, chunks)

    barrier = pltpu.get_barrier_semaphore()
    peers = [along(ll) for ll in others] + [across(pp) for pp in parts] + [sibling]
    for peer in peers:
        pl.semaphore_signal(barrier, inc=1, device_id=peer, device_id_type=MESH)
    pl.semaphore_wait(barrier, len(peers))

    sent = []

    def remote(src, dst, send, recv, device):
        return pltpu.make_async_remote_copy(
            src_ref=src, dst_ref=dst, send_sem=send, recv_sem=recv,
            device_id=device, device_id_type=MESH,
        )

    def push(src, dst, send, recv, device):
        copy = remote(src, dst, send, recv, device)
        copy.start()
        sent.append(copy)

    def arrived(dst, recv):
        remote(dst, dst, recv, recv, sibling).wait_recv()

    rhs = [rhs_ref[0, :, c * lanes : (c + 1) * lanes].astype(F32) for c in range(chunks)]

    def rhs_of(pp):
        value = rhs[0]
        for c in range(1, chunks):
            value = jnp.where(pp == c, rhs[c], value)
        return value

    def turn(step, count=1):
        def one(leaf, carry):
            turned_ref[leaf] = off_ref[leaf].reshape(slots * width, width).T
            return carry

        lax.fori_loop(step * LEAF_STEP, (step + count) * LEAF_STEP, one, 0)

    for pp in parts + [part]:
        for ll in order:
            push(
                partial_ref.at[pp, group(ll, far_base)], from_core.at[pp, group(ll)],
                core_send.at[pp, ll], core_recv.at[pp, ll], sibling,
            )

    def pair_sum(pp, f):
        return partial_ref[pp, base + f].astype(F32) + from_core[pp, f].astype(F32)

    for pp in parts:
        for ll in order:
            arrived(from_core.at[pp, group(ll)], core_recv.at[pp, ll])
            for k in range(chunks):
                f = ll * chunks + k
                value = pair_sum(pp, f)
                if ll is line:
                    value = jnp.where(part == k, value - rhs_of(pp), value)
                to_x[pp, f] = value.astype(BF16)
            push(
                to_x.at[pp, group(ll)], from_x.at[part, group(ll)],
                x_send.at[pp, ll], x_recv.at[part, ll], across(pp),
            )
    for pp in parts:
        push(panel_ref, peer_panel.at[part], panel_send.at[pp], panel_recv.at[part], across(pp))
    loads[0].wait()
    turn(0)
    totals = []
    for ll in order:
        arrived(from_core.at[part, group(ll)], core_recv.at[part, ll])
        for pp in parts:
            arrived(from_x.at[pp, group(ll)], x_recv.at[pp, ll])
        for k in range(chunks):
            f = ll * chunks + k
            value = pair_sum(part, f)
            for pp in parts:
                value += from_x[pp, f].astype(F32)
            if ll is line:
                totals.append(jnp.where(part == k, value - rhs_of(part), value))
            else:
                to_z[f] = value.astype(BF16)
        if ll is not line:
            push(to_z.at[group(ll)], from_z.at[group(line)], z_send.at[ll], z_recv.at[line], along(ll))
    turn(1)
    for ll in others:
        arrived(from_z.at[group(ll)], z_recv.at[ll])
        for k in range(chunks):
            totals[k] += from_z[ll * chunks + k].astype(F32)

    for k in range(chunks):
        gathered_in[line * chunks + k] = (-totals[k]).astype(BF16)
    mine = group(line)
    for ll in others:
        push(gathered_in.at[mine], gathered_in.at[mine], in_send.at[ll], in_recv.at[line], along(ll))

    for pp in parts:
        arrived(peer_panel.at[pp], panel_recv.at[pp])
    panels = [panel_ref] + [peer_panel.at[pp] for pp in parts]
    for f in range(fronts):
        for k, panel in enumerate(panels):
            panel_t[f * width : (f + 1) * width, k * width : (k + 1) * width] = panel[
                :, f * width : (f + 1) * width
            ].T

    turn(2)
    forward = [jnp.zeros((width, lanes), F32)] * chunks
    for ll in [line] + others:
        if ll is not line:
            arrived(gathered_in.at[group(ll)], in_recv.at[ll])
        vectors = gathered_in[group(ll)].reshape(chunks * width, lanes)
        columns = pl.ds(pl.multiple_of(ll * chunks * width, chunks * width), chunks * width)
        for k, panel in enumerate(panels):
            forward[k] += jnp.dot(panel[:, columns], vectors, preferred_element_type=F32)
    forward = [value.astype(BF16) for value in forward]
    stacked = jnp.concatenate(forward, axis=0)
    for k in range(chunks):
        gathered_fwd[line * chunks + lax.rem(part + k, chunks)] = forward[k]

    solved = None
    for ll in order:
        rows = pl.ds(pl.multiple_of(ll * chunks * width, chunks * width), chunks * width)
        term = jnp.dot(panel_t[rows, :], stacked, preferred_element_type=F32)
        if ll is line:
            solved = term
        else:
            to_adjoint[group(ll)] = term.astype(BF16).reshape(chunks, width, lanes)
            push(
                to_adjoint.at[group(ll)], from_adjoint.at[mine],
                adj_send.at[ll], adj_recv.at[line], along(ll),
            )
    steps = leaf_out.shape[0] // LEAF_STEP
    turn(3, steps - 3)
    for ll in others:
        arrived(from_adjoint.at[group(ll)], adj_recv.at[ll])
        solved += from_adjoint[group(ll)].reshape(chunks * width, lanes).astype(F32)

    def share(pp, ll):
        block = field_ref.at[pp, group(ll, base)]
        push(block, block, sib_send.at[pp, ll], sib_recv.at[pp, ll], sibling)

    def share_across(ll):
        block = field_ref.at[part, group(ll, base)]
        for pp in parts:
            push(block, block, sol_x_send.at[pp, ll], sol_x_recv.at[part, ll], across(pp))

    field_ref[part, group(line, base)] = solved.astype(BF16).reshape(chunks, width, lanes)
    own = field_ref.at[part, group(line, base)]
    for ll in others:
        push(own, own, sol_send.at[ll], sol_recv.at[line], along(ll))
    share_across(line)
    share(part, line)
    for ll in others:
        arrived(field_ref.at[part, group(ll, base)], sol_recv.at[ll])
        share_across(ll)
        share(part, ll)
    for ll in others:
        push(
            gathered_fwd.at[mine], gathered_fwd.at[mine],
            fwd_send.at[ll], fwd_recv.at[line], along(ll),
        )
    for ll in [line] + others:
        for pp in parts:
            arrived(field_ref.at[pp, group(ll, base)], sol_x_recv.at[pp, ll])
            share(pp, ll)
    for c in range(chunks):
        solution_ref[0, :, c * lanes : (c + 1) * lanes] = field_ref[c, base + me].astype(F32)

    for pp in parts + [part]:
        for ll in [line] + others:
            arrived(field_ref.at[pp, group(ll, far_base)], sib_recv.at[pp, ll])
    loads[1].wait()

    def leaf_store(step):
        some = pl.ds(step * LEAF_STEP, LEAF_STEP)
        return pltpu.make_async_copy(leaf_out.at[some], leaf_hbm.at[some], store_sems.at[step])

    def leaf_step(step, carry):
        for i in range(LEAF_STEP):
            leaf = step * LEAF_STEP + i
            picked = []
            for p in range(slots):
                row = rows_ref[p, leaf]
                block = jnp.concatenate([field_ref[c, row] for c in range(chunks)], axis=1)
                picked.append(jnp.where(p < fill_ref[leaf], block, jnp.zeros_like(block)))
            pulled = jnp.dot(
                turned_ref[leaf],
                jnp.concatenate(picked, axis=0),
                preferred_element_type=F32,
            )
            leaf_out[leaf] = (leaf_forward_ref[leaf].astype(F32) - pulled).astype(BF16)
        leaf_store(step).start()
        return carry

    lax.fori_loop(0, steps // 2, leaf_step, 0)

    for ll in others:
        arrived(gathered_fwd.at[group(ll)], fwd_recv.at[ll])

    def forward_of(sep):
        slot = jnp.int32(0)
        for p in range(fronts):
            slot = jnp.where(order_ref[0, p] == sep, p, slot)
        return gathered_fwd[slot]

    from_peer[part] = forward_of(me)
    for pp in parts:
        to_peer[pp] = forward_of(line * chunks + pp)
        push(to_peer.at[pp], from_peer.at[part], peer_send.at[pp], peer_recv.at[part], across(pp))
    lax.fori_loop(steps // 2, steps, leaf_step, 0)
    for pp in parts:
        arrived(from_peer.at[pp], peer_recv.at[pp])
    for c in range(chunks):
        forward_ref[0, :, c * lanes : (c + 1) * lanes] = from_peer[c]
    for step in range(steps):
        leaf_store(step).wait()
    for copy in sent:
        copy.wait_send()


def on_device(
    leaf_inverse, leaf_rhs, off_blocks, block_rows, fill_count, sep_rhs, panel_order, sep_inverse
):
    leaves, width = leaf_inverse.shape[:2]
    probes = leaf_rhs.shape[2]
    slots = off_blocks.shape[1]
    fronts = lax.axis_size("front")
    steps = leaves // LEAF_STEP
    block = (width, probes)
    lanes = 128
    chunks = probes // lanes
    piece = (width, lanes)
    lines = fronts // chunks
    rows = block_rows.T
    panel = sep_inverse.reshape(width, fronts * width)

    smem = pl.BlockSpec(memory_space=pltpu.SMEM)
    vmem = pl.BlockSpec(memory_space=pltpu.VMEM)
    hbm = pl.BlockSpec(memory_space=pl.ANY)
    inverse_spec = pl.BlockSpec((LEAF_STEP, width, width), lambda i: (i, 0, 0))
    vector_spec = pl.BlockSpec((LEAF_STEP,) + block, lambda i: (i, 0, 0))
    off_spec = pl.BlockSpec((LEAF_STEP, slots, width, width), lambda i: (i, 0, 0, 0))
    field_spec = pl.BlockSpec((chunks, 2 * fronts) + piece, lambda i: (0, 0, 0, 0))
    flops = 2 * leaves * (slots + 1) * width * width * probes
    moved = 2 * leaves * width * (width * (slots + 1) + 2 * probes)
    cost = pl.CostEstimate(flops=flops, bytes_accessed=moved, transcendentals=0)

    forward, partial = pl.pallas_call(
        leaf_forward,
        grid=(steps,),
        out_shape=(
            jax.ShapeDtypeStruct((leaves,) + block, BF16),
            jax.ShapeDtypeStruct((chunks, 2 * fronts) + piece, BF16),
        ),
        in_specs=[smem, smem, inverse_spec, vector_spec, off_spec],
        out_specs=(vector_spec, field_spec),
        scratch_shapes=[pltpu.VMEM((2 * fronts + 1, width // 2, lanes), F32)] * (2 * chunks),
        compiler_params=pltpu.CompilerParams(vmem_limit_bytes=VMEM_BYTES),
        cost_estimate=cost,
        name="leaf_forward",
    )(rows, fill_count, leaf_inverse, leaf_rhs, off_blocks)

    dma = pltpu.SemaphoreType.DMA
    by_line, by_both = dma((lines,)), dma((chunks, lines))
    whole = pltpu.VMEM((chunks, fronts) + piece, BF16)
    part = pltpu.VMEM((fronts,) + piece, BF16)
    small = pltpu.VMEM((chunks,) + piece, BF16)

    backward, sep_forward, sep_solution = pl.pallas_call(
        separators,
        out_shape=(
            jax.ShapeDtypeStruct((leaves,) + block, BF16),
            jax.ShapeDtypeStruct((1,) + block, BF16),
            jax.ShapeDtypeStruct((1,) + block, F32),
        ),
        in_specs=[smem, smem, smem, vmem, vmem, vmem, hbm, hbm],
        out_specs=(hbm, vmem, vmem),
        scratch_shapes=[
            pltpu.VMEM((leaves, slots, width, width), BF16),
            pltpu.VMEM((leaves, width, slots * width), BF16),
            pltpu.VMEM((leaves,) + block, BF16),
            pltpu.VMEM((leaves,) + block, BF16),
            dma((2,)), dma((steps,)),
            pltpu.VMEM((chunks, 2 * fronts) + piece, BF16),
            whole, whole, whole, part, part, part, part, part, part, small, small,
            pltpu.VMEM((fronts * width, chunks * width), BF16),
            pltpu.VMEM((chunks, width, fronts * width), BF16),
            by_both, by_both, by_both, by_both, by_line, by_line, by_line, by_line,
            by_line, by_line, by_line, by_line, by_line, by_line, by_both, by_both,
            by_both, by_both, dma((chunks,)), dma((chunks,)), dma((chunks,)), dma((chunks,)),
        ],
        compiler_params=pltpu.CompilerParams(
            collective_id=0, has_side_effects=True, vmem_limit_bytes=VMEM_BYTES
        ),
        cost_estimate=cost,
        name="separators",
    )(rows, fill_count, panel_order, partial, sep_rhs, panel, off_blocks, forward)

    one_spec = pl.BlockSpec((1,) + block, lambda i: (0, 0, 0))
    return pl.pallas_call(
        leaf_finish,
        grid=(steps,),
        out_shape=(
            jax.ShapeDtypeStruct((leaves,) + block, BF16),
            jax.ShapeDtypeStruct((1,) + block, BF16),
            jax.ShapeDtypeStruct((1,) + block, F32),
        ),
        in_specs=[inverse_spec, vector_spec, one_spec, one_spec],
        out_specs=(vector_spec, one_spec, one_spec),
        compiler_params=pltpu.CompilerParams(vmem_limit_bytes=VMEM_BYTES),
        cost_estimate=cost,
        name="leaf_finish",
    )(leaf_inverse, backward, sep_forward, sep_solution)


def solution(mesh):
    placed = (
        P(("leaf", "front"), None, None),
        P(("leaf", "front"), None, None),
        P(("leaf", "front"), None, None, None),
        P(("leaf", "front"), None),
        P(("leaf", "front")),
        P(("leaf", "front"), None, None),
        P("leaf", None),
        P(("leaf", "front"), None, None),
    )
    return jax.shard_map(
        on_device,
        mesh=mesh,
        in_specs=placed,
        out_specs=(
            P(("leaf", "front"), None, None),
            P(("leaf", "front"), None, None),
            P(("leaf", "front"), None, None),
        ),
        check_vma=False,
    )
```

```python
import jax
import jax.numpy as jnp
from jax import lax
from jax.experimental import pallas as pl
from jax.experimental.pallas import tpu as pltpu
from jax.sharding import PartitionSpec as P

MESH = pl.DeviceIdType.MESH
F32 = jnp.float32
BF16 = jnp.bfloat16
LEAF_STEP = 8
FIRST_DIMS = (((0,), (0,)), ((), ()))
VMEM_BYTES = 56 * 1024 * 1024


def leaf_forward(
    rows_ref, fill_ref, inverse_ref, rhs_ref, off_ref, forward_ref, partial_ref, *accs
):
    step = pl.program_id(0)
    chunks, seps, _, lanes = partial_ref.shape
    slots, width = off_ref.shape[1], off_ref.shape[2]
    bands = len(accs) // chunks
    band = width // bands

    @pl.when(step == 0)
    def _():
        for acc in accs:
            acc[...] = jnp.zeros_like(acc)

    for i in range(LEAF_STEP):
        forward_ref[i] = jnp.dot(
            inverse_ref[i], rhs_ref[i], preferred_element_type=F32
        ).astype(BF16)
    for i in range(LEAF_STEP):
        leaf = step * LEAF_STEP + i
        stacked = off_ref[i].reshape(slots * width, width)
        product = jnp.dot(stacked, forward_ref[i], preferred_element_type=F32)
        for p in range(slots):
            target = jnp.where(p < fill_ref[leaf], rows_ref[p, leaf], seps)
            for k, acc in enumerate(accs):
                c, top = k % chunks, p * width + k // chunks * band
                acc[target] += product[top : top + band, c * lanes : (c + 1) * lanes]

    @pl.when(step == pl.num_programs(0) - 1)
    def _():
        for k, acc in enumerate(accs):
            top = k // chunks * band
            partial_ref[k % chunks, :, top : top + band, :] = acc[:seps].astype(BF16)


def leaf_finish(
    inverse_ref, backward_ref, sep_fwd_ref, sep_sol_ref, out_ref, sep_fwd_out, sep_sol_out
):
    @pl.when(pl.program_id(0) == 0)
    def _():
        sep_fwd_out[...] = sep_fwd_ref[...]
        sep_sol_out[...] = sep_sol_ref[...]

    for i in range(LEAF_STEP):
        out_ref[i] = lax.dot_general(
            inverse_ref[i], backward_ref[i], FIRST_DIMS, preferred_element_type=F32
        ).astype(BF16)


def separators(
    rows_ref, fill_ref, order_ref, partial_ref, rhs_ref, panel_ref, off_hbm, leaf_forward_hbm,
    leaf_hbm, forward_ref, solution_ref,
    off_ref, turned_ref, leaf_forward_ref, leaf_out, load_sems, store_sems, field_ref,
    from_core, to_x, from_x, to_z, from_z, gathered_in, to_adjoint, from_adjoint, gathered_fwd,
    to_peer, from_peer, panel_t, peer_panel,
    core_send, core_recv, x_send, x_recv, z_send, z_recv, in_send, in_recv, adj_send, adj_recv,
    fwd_send, fwd_recv, sol_send, sol_recv, sol_x_send, sol_x_recv, sib_send, sib_recv,
    peer_send, peer_recv, panel_send, panel_recv,
):
    loads = [
        pltpu.make_async_copy(off_hbm, off_ref, load_sems.at[0]),
        pltpu.make_async_copy(leaf_forward_hbm, leaf_forward_ref, load_sems.at[1]),
    ]
    for load in loads:
        load.start()
    chunks, seps, width, lanes = partial_ref.shape
    slots = rows_ref.shape[0]
    fronts = seps // 2
    lines = fronts // chunks
    leaf, me = lax.axis_index("leaf"), lax.axis_index("front")
    half = lax.rem(leaf, 2)
    line, part = me // chunks, lax.rem(me, chunks)
    base, far_base = half * fronts, (1 - half) * fronts
    sibling = (leaf + 1 - 2 * half, me)
    others = [lax.rem(line + k, lines) for k in range(1, lines)]
    parts = [lax.rem(part + k, chunks) for k in range(1, chunks)]
    order = others + [line]

    def along(ll):
        return (leaf, ll * chunks + part)

    def across(pp):
        return (leaf, line * chunks + pp)

    def group(ll, start=0):
        return pl.ds(start + ll * chunks, chunks)

    barrier = pltpu.get_barrier_semaphore()
    peers = [along(ll) for ll in others] + [across(pp) for pp in parts] + [sibling]
    for peer in peers:
        pl.semaphore_signal(barrier, inc=1, device_id=peer, device_id_type=MESH)
    pl.semaphore_wait(barrier, len(peers))

    sent = []

    def remote(src, dst, send, recv, device):
        return pltpu.make_async_remote_copy(
            src_ref=src, dst_ref=dst, send_sem=send, recv_sem=recv,
            device_id=device, device_id_type=MESH,
        )

    def push(src, dst, send, recv, device):
        copy = remote(src, dst, send, recv, device)
        copy.start()
        sent.append(copy)

    def arrived(dst, recv):
        remote(dst, dst, recv, recv, sibling).wait_recv()

    rhs = [rhs_ref[0, :, c * lanes : (c + 1) * lanes].astype(F32) for c in range(chunks)]

    def rhs_of(pp):
        value = rhs[0]
        for c in range(1, chunks):
            value = jnp.where(pp == c, rhs[c], value)
        return value

    def turn(step, count=1):
        def one(leaf, carry):
            turned_ref[leaf] = off_ref[leaf].reshape(slots * width, width).T
            return carry

        lax.fori_loop(step * LEAF_STEP, (step + count) * LEAF_STEP, one, 0)

    for pp in parts + [part]:
        for ll in order:
            push(
                partial_ref.at[pp, group(ll, far_base)], from_core.at[pp, group(ll)],
                core_send.at[pp, ll], core_recv.at[pp, ll], sibling,
            )

    def pair_sum(pp, f):
        return partial_ref[pp, base + f].astype(F32) + from_core[pp, f].astype(F32)

    for pp in parts:
        for ll in order:
            arrived(from_core.at[pp, group(ll)], core_recv.at[pp, ll])
            for k in range(chunks):
                f = ll * chunks + k
                value = pair_sum(pp, f)
                if ll is line:
                    value = jnp.where(part == k, value - rhs_of(pp), value)
                to_x[pp, f] = value.astype(BF16)
            push(
                to_x.at[pp, group(ll)], from_x.at[part, group(ll)],
                x_send.at[pp, ll], x_recv.at[part, ll], across(pp),
            )
    for pp in parts:
        push(panel_ref, peer_panel.at[part], panel_send.at[pp], panel_recv.at[part], across(pp))
    totals = []
    for ll in order:
        arrived(from_core.at[part, group(ll)], core_recv.at[part, ll])
        for pp in parts:
            arrived(from_x.at[pp, group(ll)], x_recv.at[pp, ll])
        for k in range(chunks):
            f = ll * chunks + k
            value = pair_sum(part, f)
            for pp in parts:
                value += from_x[pp, f].astype(F32)
            if ll is line:
                totals.append(jnp.where(part == k, value - rhs_of(part), value))
            else:
                to_z[f] = value.astype(BF16)
        if ll is not line:
            push(to_z.at[group(ll)], from_z.at[group(line)], z_send.at[ll], z_recv.at[line], along(ll))
    for ll in others:
        arrived(from_z.at[group(ll)], z_recv.at[ll])
        for k in range(chunks):
            totals[k] += from_z[ll * chunks + k].astype(F32)

    for k in range(chunks):
        gathered_in[line * chunks + k] = (-totals[k]).astype(BF16)
    mine = group(line)
    for ll in others:
        push(gathered_in.at[mine], gathered_in.at[mine], in_send.at[ll], in_recv.at[line], along(ll))

    for pp in parts:
        arrived(peer_panel.at[pp], panel_recv.at[pp])
    panels = [panel_ref] + [peer_panel.at[pp] for pp in parts]
    for f in range(fronts):
        for k, panel in enumerate(panels):
            panel_t[f * width : (f + 1) * width, k * width : (k + 1) * width] = panel[
                :, f * width : (f + 1) * width
            ].T

    steps = leaf_out.shape[0] // LEAF_STEP
    loads[0].wait()
    turn(0, steps // 2)
    forward = [jnp.zeros((width, lanes), F32)] * chunks
    for ll in [line] + others:
        if ll is not line:
            arrived(gathered_in.at[group(ll)], in_recv.at[ll])
        vectors = gathered_in[group(ll)].reshape(chunks * width, lanes)
        columns = pl.ds(pl.multiple_of(ll * chunks * width, chunks * width), chunks * width)
        for k, panel in enumerate(panels):
            forward[k] += jnp.dot(panel[:, columns], vectors, preferred_element_type=F32)
    forward = [value.astype(BF16) for value in forward]
    stacked = jnp.concatenate(forward, axis=0)
    for k in range(chunks):
        gathered_fwd[line * chunks + lax.rem(part + k, chunks)] = forward[k]

    solved = None
    for ll in order:
        rows = pl.ds(pl.multiple_of(ll * chunks * width, chunks * width), chunks * width)
        term = jnp.dot(panel_t[rows, :], stacked, preferred_element_type=F32)
        if ll is line:
            solved = term
        else:
            to_adjoint[group(ll)] = term.astype(BF16).reshape(chunks, width, lanes)
            push(
                to_adjoint.at[group(ll)], from_adjoint.at[mine],
                adj_send.at[ll], adj_recv.at[line], along(ll),
            )
    turn(steps // 2, steps - steps // 2)
    for ll in others:
        arrived(from_adjoint.at[group(ll)], adj_recv.at[ll])
        solved += from_adjoint[group(ll)].reshape(chunks * width, lanes).astype(F32)

    def share(pp, ll):
        block = field_ref.at[pp, group(ll, base)]
        push(block, block, sib_send.at[pp, ll], sib_recv.at[pp, ll], sibling)

    def share_across(ll):
        block = field_ref.at[part, group(ll, base)]
        for pp in parts:
            push(block, block, sol_x_send.at[pp, ll], sol_x_recv.at[part, ll], across(pp))

    field_ref[part, group(line, base)] = solved.astype(BF16).reshape(chunks, width, lanes)
    own = field_ref.at[part, group(line, base)]
    for ll in others:
        push(own, own, sol_send.at[ll], sol_recv.at[line], along(ll))
    share_across(line)
    share(part, line)
    for ll in others:
        arrived(field_ref.at[part, group(ll, base)], sol_recv.at[ll])
        share_across(ll)
        share(part, ll)
    for ll in others:
        push(
            gathered_fwd.at[mine], gathered_fwd.at[mine],
            fwd_send.at[ll], fwd_recv.at[line], along(ll),
        )
    for ll in [line] + others:
        for pp in parts:
            arrived(field_ref.at[pp, group(ll, base)], sol_x_recv.at[pp, ll])
            share(pp, ll)
    for c in range(chunks):
        solution_ref[0, :, c * lanes : (c + 1) * lanes] = field_ref[c, base + me].astype(F32)

    for pp in parts + [part]:
        for ll in [line] + others:
            arrived(field_ref.at[pp, group(ll, far_base)], sib_recv.at[pp, ll])
    loads[1].wait()

    def leaf_store(step):
        some = pl.ds(step * LEAF_STEP, LEAF_STEP)
        return pltpu.make_async_copy(leaf_out.at[some], leaf_hbm.at[some], store_sems.at[step])

    def leaf_step(step, carry):
        for i in range(LEAF_STEP):
            leaf = step * LEAF_STEP + i
            picked = []
            for p in range(slots):
                row = rows_ref[p, leaf]
                block = jnp.concatenate([field_ref[c, row] for c in range(chunks)], axis=1)
                picked.append(jnp.where(p < fill_ref[leaf], block, jnp.zeros_like(block)))
            pulled = jnp.dot(
                turned_ref[leaf],
                jnp.concatenate(picked, axis=0),
                preferred_element_type=F32,
            )
            leaf_out[leaf] = (leaf_forward_ref[leaf].astype(F32) - pulled).astype(BF16)
        leaf_store(step).start()
        return carry

    lax.fori_loop(0, steps // 2, leaf_step, 0)

    for ll in others:
        arrived(gathered_fwd.at[group(ll)], fwd_recv.at[ll])

    def forward_of(sep):
        slot = jnp.int32(0)
        for p in range(fronts):
            slot = jnp.where(order_ref[0, p] == sep, p, slot)
        return gathered_fwd[slot]

    from_peer[part] = forward_of(me)
    for pp in parts:
        to_peer[pp] = forward_of(line * chunks + pp)
        push(to_peer.at[pp], from_peer.at[part], peer_send.at[pp], peer_recv.at[part], across(pp))
    lax.fori_loop(steps // 2, steps, leaf_step, 0)
    for pp in parts:
        arrived(from_peer.at[pp], peer_recv.at[pp])
    for c in range(chunks):
        forward_ref[0, :, c * lanes : (c + 1) * lanes] = from_peer[c]
    for step in range(steps):
        leaf_store(step).wait()
    for copy in sent:
        copy.wait_send()


def on_device(
    leaf_inverse, leaf_rhs, off_blocks, block_rows, fill_count, sep_rhs, panel_order, sep_inverse
):
    leaves, width = leaf_inverse.shape[:2]
    probes = leaf_rhs.shape[2]
    slots = off_blocks.shape[1]
    fronts = lax.axis_size("front")
    steps = leaves // LEAF_STEP
    block = (width, probes)
    lanes = 128
    chunks = probes // lanes
    piece = (width, lanes)
    lines = fronts // chunks
    rows = block_rows.T
    panel = sep_inverse.reshape(width, fronts * width)

    smem = pl.BlockSpec(memory_space=pltpu.SMEM)
    vmem = pl.BlockSpec(memory_space=pltpu.VMEM)
    hbm = pl.BlockSpec(memory_space=pl.ANY)
    inverse_spec = pl.BlockSpec((LEAF_STEP, width, width), lambda i: (i, 0, 0))
    vector_spec = pl.BlockSpec((LEAF_STEP,) + block, lambda i: (i, 0, 0))
    off_spec = pl.BlockSpec((LEAF_STEP, slots, width, width), lambda i: (i, 0, 0, 0))
    field_spec = pl.BlockSpec((chunks, 2 * fronts) + piece, lambda i: (0, 0, 0, 0))
    flops = 2 * leaves * (slots + 1) * width * width * probes
    moved = 2 * leaves * width * (width * (slots + 1) + 2 * probes)
    cost = pl.CostEstimate(flops=flops, bytes_accessed=moved, transcendentals=0)

    forward, partial = pl.pallas_call(
        leaf_forward,
        grid=(steps,),
        out_shape=(
            jax.ShapeDtypeStruct((leaves,) + block, BF16),
            jax.ShapeDtypeStruct((chunks, 2 * fronts) + piece, BF16),
        ),
        in_specs=[smem, smem, inverse_spec, vector_spec, off_spec],
        out_specs=(vector_spec, field_spec),
        scratch_shapes=[pltpu.VMEM((2 * fronts + 1, width // 2, lanes), F32)] * (2 * chunks),
        compiler_params=pltpu.CompilerParams(vmem_limit_bytes=VMEM_BYTES),
        cost_estimate=cost,
        name="leaf_forward",
    )(rows, fill_count, leaf_inverse, leaf_rhs, off_blocks)

    dma = pltpu.SemaphoreType.DMA
    by_line, by_both = dma((lines,)), dma((chunks, lines))
    whole = pltpu.VMEM((chunks, fronts) + piece, BF16)
    part = pltpu.VMEM((fronts,) + piece, BF16)
    small = pltpu.VMEM((chunks,) + piece, BF16)

    backward, sep_forward, sep_solution = pl.pallas_call(
        separators,
        out_shape=(
            jax.ShapeDtypeStruct((leaves,) + block, BF16),
            jax.ShapeDtypeStruct((1,) + block, BF16),
            jax.ShapeDtypeStruct((1,) + block, F32),
        ),
        in_specs=[smem, smem, smem, vmem, vmem, vmem, hbm, hbm],
        out_specs=(hbm, vmem, vmem),
        scratch_shapes=[
            pltpu.VMEM((leaves, slots, width, width), BF16),
            pltpu.VMEM((leaves, width, slots * width), BF16),
            pltpu.VMEM((leaves,) + block, BF16),
            pltpu.VMEM((leaves,) + block, BF16),
            dma((2,)), dma((steps,)),
            pltpu.VMEM((chunks, 2 * fronts) + piece, BF16),
            whole, whole, whole, part, part, part, part, part, part, small, small,
            pltpu.VMEM((fronts * width, chunks * width), BF16),
            pltpu.VMEM((chunks, width, fronts * width), BF16),
            by_both, by_both, by_both, by_both, by_line, by_line, by_line, by_line,
            by_line, by_line, by_line, by_line, by_line, by_line, by_both, by_both,
            by_both, by_both, dma((chunks,)), dma((chunks,)), dma((chunks,)), dma((chunks,)),
        ],
        compiler_params=pltpu.CompilerParams(
            collective_id=0, has_side_effects=True, vmem_limit_bytes=VMEM_BYTES
        ),
        cost_estimate=cost,
        name="separators",
    )(rows, fill_count, panel_order, partial, sep_rhs, panel, off_blocks, forward)

    one_spec = pl.BlockSpec((1,) + block, lambda i: (0, 0, 0))
    return pl.pallas_call(
        leaf_finish,
        grid=(steps,),
        out_shape=(
            jax.ShapeDtypeStruct((leaves,) + block, BF16),
            jax.ShapeDtypeStruct((1,) + block, BF16),
            jax.ShapeDtypeStruct((1,) + block, F32),
        ),
        in_specs=[inverse_spec, vector_spec, one_spec, one_spec],
        out_specs=(vector_spec, one_spec, one_spec),
        compiler_params=pltpu.CompilerParams(vmem_limit_bytes=VMEM_BYTES),
        cost_estimate=cost,
        name="leaf_finish",
    )(leaf_inverse, backward, sep_forward, sep_solution)


def solution(mesh):
    placed = (
        P(("leaf", "front"), None, None),
        P(("leaf", "front"), None, None),
        P(("leaf", "front"), None, None, None),
        P(("leaf", "front"), None),
        P(("leaf", "front")),
        P(("leaf", "front"), None, None),
        P("leaf", None),
        P(("leaf", "front"), None, None),
    )
    return jax.shard_map(
        on_device,
        mesh=mesh,
        in_specs=placed,
        out_specs=(
            P(("leaf", "front"), None, None),
            P(("leaf", "front"), None, None),
            P(("leaf", "front"), None, None),
        ),
        check_vma=False,
    )
```
